256 devices in a mesh: seq: 16 (over z, x_hi), kvh: 2 (over core), batch: 8 (over x_lo, y).
Axes of the slice: x: 4 (x_hi: 2, x_lo: 2; x = x_hi * 2 + x_lo), y: 4, z: 8, core: 2. Of those that a mesh axis runs over, the one named last changes fastest.
Arguments:
- queries: bfloat16 [32, 1024, 3584], P('batch', 'seq', 'kvh'), parts along dimension 0, may hold values from -160 to 160
- text_keys: bfloat16 [32, 1024, 512], P('batch', 'seq', 'kvh'), parts along dimension 0, may hold values from -6 to 6
- text_values: bfloat16 [32, 1024, 512], P('batch', 'seq', 'kvh'), parts along dimension 0, may hold values from -6 to 6
- visual_keys: bfloat16 [128, 729, 512], P(('batch', 'seq'), None, 'kvh'), parts along dimension 0, may hold values from -6 to 6
- visual_values: bfloat16 [128, 729, 512], P(('batch', 'seq'), None, 'kvh'), parts along dimension 0, may hold values from -6 to 6
- gate_weight: float32 [3584, 28], P('kvh'), may hold values from -0.1875 to 0.1875
- text_offsets: int32 [128], P('batch'), parts along dimension 0, may hold values from 0 to 960, as said below
- image_sequence: int32 [128], P('batch'), parts along dimension 0, may hold values from 0 to 3, as said below
- image_position: int32 [128], P('batch'), parts along dimension 0, may hold values from 0 to 1023, as said below
Outputs:
- combined: bfloat16 [32, 1024, 3584], P('batch', 'seq', 'kvh'), parts along dimension 0
The draws below stay inside these ranges and needn't reach their ends.
There are 8 independent parts, one for each index of `batch`. The reference program is written for one: setup_inputs(seed, part) draws one part's arguments, and reference() takes and returns one part's arrays. A program takes and returns all parts, laid end to end along the dimension named above; an argument that names none is the same for every part. Nothing has to cross between parts.
Inputs may be any that keep to these rules, and one draw needn't show every extreme that they name: A permutation of the multiples of 64 below 1024: text block j holds the positions text_offsets[j] to text_offsets[j] + 63. `image_sequence`: each of the 4 sequences owns exactly 4 images. `image_position`: every sequence has an image at position 0.
All inputs are finite; a program needn't handle non-finite values.
Results may differ from the reference program's by a relative error of at most 0.0039.
Values may be sent and summed in bfloat16 or wider, within the bound.
No kernel may reach another device: no remote copies, remote signals or barrier semaphores. Data moves between devices by JAX's collectives and lax.ppermute only.
A program may use at most 128 MiB of HBM per device.

```python
import jax
import jax.numpy as jnp
from jax import lax

HQ = 28
KVH = 4
DH = 128
VTOK = 729
TOK_DEV = 64
SEQS = 4
IMG_SEQ = 4
GROUP = 7
SHARDS = 16
L = 1024
IMAGES = 16


def layout_order(key):
    return jax.random.permutation(jax.random.fold_in(key, 101), SHARDS).astype(jnp.int32)


def image_plan(key):
    shuffled = jax.random.permutation(jax.random.fold_in(key, 202), IMAGES).astype(jnp.int32)
    owners = (shuffled % SEQS).astype(jnp.int32)
    places = jax.random.randint(jax.random.fold_in(key, 203), (IMAGES,), 1, L, dtype=jnp.int32)
    places = jnp.where(shuffled < SEQS, 0, places).astype(jnp.int32)
    return (owners, places)


def text_key_base(key):
    return jnp.clip(jax.random.normal(jax.random.fold_in(key, 11), (SEQS, L, KVH * DH), jnp.float32), -6.0, 6.0)


def visual_key_base(key):
    return jnp.clip(jax.random.normal(jax.random.fold_in(key, 12), (IMAGES, VTOK, KVH * DH), jnp.float32), -6.0, 6.0)


def draw_text_offsets(key, part):
    return (layout_order(key) * TOK_DEV).astype(jnp.int32)


def draw_image_sequence(key, part):
    return image_plan(key)[0]


def draw_image_position(key, part):
    return image_plan(key)[1]


def draw_text_keys(key, part):
    drawn = text_key_base(key)
    return drawn.astype(jnp.bfloat16)


def draw_visual_keys(key, part):
    drawn = visual_key_base(key)
    return drawn.astype(jnp.bfloat16)


def draw_queries(key, part):
    drawn = jnp.clip(jax.random.normal(jax.random.fold_in(key, 13), (SEQS, L, HQ * DH), jnp.float32), -6.0, 6.0)
    return drawn.astype(jnp.bfloat16)


def steps_of(rng, dims, cuts, smallest, largest):
    level, own = 1.0, jax.random.fold_in(rng, 6)
    for dim, blocks in cuts:
        draws = jnp.exp(jax.random.uniform(jax.random.fold_in(own, dim), (blocks,), jnp.float32, smallest / len(cuts), largest / len(cuts)))
        level = level * jnp.repeat(draws, dims[dim] // blocks).reshape([-1 if axis == dim else 1 for axis in range(len(dims))])
    return level


def gaussian(own_key, extent, width, bound, pieces=(), kind=jnp.bfloat16):
    values = width * jax.random.normal(own_key, extent, jnp.float32)
    if pieces:
        values = values * steps_of(own_key, extent, pieces, -0.22, 0.18)
    return jnp.clip(values, -bound, bound).astype(kind)


def setup_inputs(seed: int = 0, part: int = 0) -> dict:
    arg_keys = jax.random.split(jax.random.key(seed), 10)
    part_splits = jax.random.split(jax.random.fold_in(arg_keys[9], part), 10)
    return {
        "queries": draw_queries(jax.random.fold_in(jax.random.fold_in(arg_keys[9], part), 71), part),
        "text_keys": draw_text_keys(jax.random.fold_in(jax.random.fold_in(arg_keys[9], part), 71), part),
        "text_values": gaussian(part_splits[2], (SEQS, L, KVH * DH), 1.0, 6.0, ((1, 16), (2, 2))),
        "visual_keys": draw_visual_keys(jax.random.fold_in(jax.random.fold_in(arg_keys[9], part), 71), part),
        "visual_values": gaussian(part_splits[4], (IMAGES, VTOK, KVH * DH), 1.0, 6.0, ((0, 16), (2, 2))),
        "gate_weight": gaussian(arg_keys[5], (HQ * DH, HQ), (HQ * DH // 4) ** -0.5, 0.1875, ((0, 2),), jnp.float32),
        "text_offsets": draw_text_offsets(jax.random.fold_in(jax.random.fold_in(arg_keys[9], part), 71), part),
        "image_sequence": draw_image_sequence(jax.random.fold_in(jax.random.fold_in(arg_keys[9], part), 71), part),
        "image_position": draw_image_position(jax.random.fold_in(jax.random.fold_in(arg_keys[9], part), 71), part),
    }


NEG = -1.0e30


def block_stats(query_rows, key_blocks, value_blocks, visible):
    scaling = 1.0 / (query_rows.shape[-1] ** 0.5)
    scores = jnp.einsum("tghe,bkge->tghbk", query_rows.astype(jnp.float32), key_blocks.astype(jnp.float32), precision=lax.Precision.HIGHEST) * scaling
    allowed = visible[:, None, None, :, :]
    scores = jnp.where(allowed, scores, NEG)
    block_peak = jnp.max(scores, axis=-1)
    unnormed = jnp.where(allowed, jnp.exp(scores - block_peak[..., None]), 0.0)
    block_total = jnp.sum(unnormed, axis=-1)
    rounded = lax.optimization_barrier(unnormed.astype(jnp.bfloat16)).astype(jnp.float32)
    block_sum = jnp.einsum("tghbk,bkge->tghbe", rounded, value_blocks.astype(jnp.float32), precision=lax.Precision.HIGHEST)
    return block_peak, block_total, block_sum


def finish(block_peak, block_total, block_sum):
    overall = jnp.max(block_peak, axis=-1)
    weights = jnp.exp(block_peak - overall[..., None])
    numerator = jnp.sum(weights[..., None] * block_sum, axis=-2)
    denominator = jnp.sum(weights * block_total, axis=-1)
    return numerator / denominator[..., None]


def reference(queries, text_keys, text_values, visual_keys, visual_values, gate_weight, text_offsets, image_sequence, image_position):
    length = queries.shape[1]
    shaped = queries.reshape(SEQS, length, KVH, GROUP, DH)
    rows_all = jnp.arange(length, dtype=jnp.int32)
    positions = (text_offsets[rows_all // TOK_DEV] + rows_all % TOK_DEV).astype(jnp.int32)
    gate_logits = jnp.dot(queries.astype(jnp.float32).reshape(SEQS * length, HQ * DH), gate_weight, precision=lax.Precision.HIGHEST)
    gate = jax.nn.sigmoid(gate_logits).reshape(SEQS, length, KVH, GROUP)
    key_pos = (text_offsets[:, None] + jnp.arange(TOK_DEV, dtype=jnp.int32)[None, :]).astype(jnp.int32)
    text_visible = key_pos[None, :, :] <= positions[:, None, None]
    key_blocks = text_keys.reshape(SEQS, SHARDS, TOK_DEV, KVH, DH)
    value_blocks = text_values.reshape(SEQS, SHARDS, TOK_DEV, KVH, DH)

    def text_one(members):
        query_rows, keys_here, values_here = members
        return finish(*block_stats(query_rows, keys_here, values_here, text_visible))

    text_out = lax.map(text_one, (shaped, key_blocks, value_blocks))
    order = jnp.argsort(image_sequence, stable=True).reshape(SEQS, IMG_SEQ)
    image_keys = visual_keys.reshape(IMAGES, VTOK, KVH, DH)[order]
    image_values = visual_values.reshape(IMAGES, VTOK, KVH, DH)[order]
    image_places = image_position[order]

    def visual_one(members):
        query_rows, keys_here, values_here, places_here = members
        visible = jnp.broadcast_to(places_here[None, :, None] <= positions[:, None, None], (length, IMG_SEQ, VTOK))
        return finish(*block_stats(query_rows, keys_here, values_here, visible))

    visual_out = lax.map(visual_one, (shaped, image_keys, image_values, image_places))
    mixed = (1.0 - gate)[..., None] * text_out + gate[..., None] * visual_out
    return mixed.reshape(SEQS, length, HQ * DH).astype(jnp.bfloat16)
```

```python
import functools

import jax
import jax.numpy as jnp
from jax import lax
from jax.experimental import pallas as pl
from jax.experimental.pallas import tpu as pltpu
from jax.sharding import Mesh, PartitionSpec as P

HQ = 28
DH = 128
GROUP = 7
SEQS = 4
ROWS = 64
WIDE = GROUP * DH
VTOK = 729
VROWS = 736
VPAD = 768
TEXT = SEQS * ROWS
CHUNK = TEXT + VROWS
PLANES = 8
NEG = -1e30
EXP_SCALE = 1.4426950408889634 / DH**0.5

Z, X, OFFSET, OWNER, PLACE, SLOT = 0, 1, 2, 18, 34, 50

VMEM_BYTES = 40 * 1024 * 1024


def source(plan, hop):
    plane, stream = hop
    z = lax.rem(plan[Z] + (plane + PLANES), PLANES)
    x = plan[X] if stream == 0 else 1 - plan[X]
    return 2 * z + x


def pick(step, options):
    value = options[0]
    for i in range(1, len(options)):
        value = jnp.where(step == i, options[i], value)
    return value


def params(flops, bytes_accessed, exps, **more):
    return dict(
        compiler_params=pltpu.CompilerParams(vmem_limit_bytes=VMEM_BYTES, **more),
        cost_estimate=pl.CostEstimate(
            flops=flops, bytes_accessed=bytes_accessed, transcendentals=exps
        ),
    )


def stack_heads(qa, qb):
    parts = []
    for h in range(GROUP):
        cols = slice(h * DH, (h + 1) * DH)
        parts += [qa[:, cols], qb[:, cols]]
    return jnp.concatenate(parts, axis=0)


def query_positions(plan):
    rows = lax.broadcasted_iota(jnp.int32, (2 * ROWS, 1), 0)
    own = plan[OFFSET + 2 * plan[Z] + plan[X]]
    other = plan[OFFSET + 2 * plan[Z] + 1 - plan[X]]
    return jnp.where(rows < ROWS, own + rows, other + rows - ROWS)


def pack_stats(peaks, totals):
    lanes = lax.broadcasted_iota(jnp.int32, (2 * ROWS, DH), 1)
    stats = jnp.zeros((2 * ROWS, DH), jnp.float32)
    for h in range(GROUP):
        stats = jnp.where(lanes == h, peaks[h], stats)
        stats = jnp.where(lanes == 8 + h, totals[h], stats)
    return stats


def pack_body(plan, tk, tv, vk, vv, q, own, other, q_other):
    for ref, g in ((own, plan[X]), (other, 1 - plan[X])):
        cols = pl.ds(pl.multiple_of(g * DH, DH), DH)
        for s in range(SEQS):
            ref[s * ROWS : (s + 1) * ROWS, :DH] = tk[s, :, cols]
            ref[s * ROWS : (s + 1) * ROWS, DH:] = tv[s, :, cols]
        ref[CHUNK - 16 :, :] = jnp.zeros((16, 2 * DH), jnp.bfloat16)
        ref[TEXT : TEXT + VTOK, :DH] = vk[0, :, cols]
        ref[TEXT : TEXT + VTOK, DH:] = vv[0, :, cols]
    q_other[...] = q[...]


def pack(plan, tk, tv, vk, vv, q):
    full = lambda a: pl.BlockSpec(a.shape, lambda i, plan, n=a.ndim: (0,) * n)
    chunk = jax.ShapeDtypeStruct((CHUNK, 2 * DH), jnp.bfloat16)
    half = (SEQS, ROWS, WIDE)
    return pl.pallas_call(
        pack_body,
        grid_spec=pltpu.PrefetchScalarGridSpec(
            num_scalar_prefetch=1,
            grid=(1,),
            in_specs=[full(tk), full(tv), full(vk), full(vv)]
            + [pl.BlockSpec(half, lambda i, plan: (0, 0, 1 - plan[X]))],
            out_specs=[full(chunk), full(chunk), pl.BlockSpec(half, lambda i, plan: (0, 0, 0))],
        ),
        out_shape=[chunk, chunk, jax.ShapeDtypeStruct(half, jnp.bfloat16)],
        name="pack",
        **params(0, 3_000_000, 0),
    )(plan, tk, tv, vk, vv, q)


def gate_body(q, w, out):
    total = w[...]
    hi = total.astype(jnp.bfloat16)
    rest = total - hi.astype(jnp.float32)
    mid = rest.astype(jnp.bfloat16)
    low = (rest - mid.astype(jnp.float32)).astype(jnp.bfloat16)
    rows = q[...].reshape(SEQS * ROWS, q.shape[-1])
    acc = jnp.dot(rows, low, preferred_element_type=jnp.float32)
    acc += jnp.dot(rows, mid, preferred_element_type=jnp.float32)
    acc += jnp.dot(rows, hi, preferred_element_type=jnp.float32)
    out[...] = acc.reshape(SEQS, ROWS, HQ)


def gate_share(q, w):
    return pl.pallas_call(
        gate_body,
        out_shape=jax.ShapeDtypeStruct((SEQS, ROWS, HQ), jnp.float32),
        name="gate_share",
        **params(100_000_000, 1_200_000, 0),
    )(q, w)


def image_body(hops, plan, *refs):
    n = len(hops)
    chunks = refs[:n]
    qa, qb = refs[n], refs[n + 1]
    refs = refs[n + 2 :]
    out, stat, keys, values = refs[-4:]
    step = pl.program_id(0)

    @pl.when(step == 0)
    def _():
        values[:, DH:] = jnp.ones((VPAD, DH), jnp.bfloat16)
        values[VROWS:, :DH] = jnp.zeros((VPAD - VROWS, DH), jnp.bfloat16)
        keys[VROWS:, :] = jnp.zeros((VPAD - VROWS, DH), jnp.bfloat16)

    for i in range(n):

        @pl.when(step == i)
        def _(i=i):
            keys[:VROWS, :] = chunks[i][TEXT:, :DH]
            values[:VROWS, :DH] = chunks[i][TEXT:, DH:]

    place = pick(step, [plan[PLACE + source(plan, hop)] for hop in hops])
    visible = query_positions(plan) >= place
    query = stack_heads(qa[0], qb[0])
    k, v = keys[...], values[...]
    scores = lax.dot_general(
        query, k, (((1,), (1,)), ((), ())), preferred_element_type=jnp.float32
    )
    lanes = lax.broadcasted_iota(jnp.int32, (1, DH), 1)
    edge = jnp.where(lanes < VTOK - (VPAD - DH), scores[:, VPAD - DH :], NEG)
    scores = jnp.concatenate([scores[:, : VPAD - DH], edge], axis=1)
    peak = jnp.max(scores, axis=1, keepdims=True)
    weights = jnp.exp2((scores - peak) * EXP_SCALE).astype(jnp.bfloat16)
    summed = jnp.dot(weights, v, preferred_element_type=jnp.float32)
    peaks, totals = [], []
    for h in range(GROUP):
        rows = slice(h * 2 * ROWS, (h + 1) * 2 * ROWS)
        out[0, :, h * DH : (h + 1) * DH] = summed[rows, :DH]
        peaks.append(jnp.where(visible, peak[rows], NEG))
        totals.append(summed[rows, DH:])
    stat[0] = pack_stats(peaks, totals)


PARTIAL = jax.ShapeDtypeStruct((4 * SEQS, 2 * ROWS, WIDE), jnp.float32)
STATS = jax.ShapeDtypeStruct((4 * SEQS, 2 * ROWS, DH), jnp.float32)


def image_part(plan, hops, chunks, q, q_in, held):
    n = len(hops)

    def owner(i, plan):
        return pick(i, [plan[OWNER + source(plan, hop)] for hop in hops])

    def slot(i, plan):
        return (pick(i, [plan[SLOT + source(plan, hop)] for hop in hops]), 0, 0)

    in_specs = [pl.BlockSpec((CHUNK, 2 * DH), lambda i, plan: (0, 0))] * n + [
        pl.BlockSpec((1, ROWS, WIDE), lambda i, plan: (owner(i, plan), 0, plan[X])),
        pl.BlockSpec((1, ROWS, WIDE), lambda i, plan: (owner(i, plan), 0, 0)),
    ]
    aliases = {}
    if held:
        in_specs += [pl.BlockSpec(memory_space=pl.ANY)] * 2
        aliases = {n + 3: 0, n + 4: 1}
    return pl.pallas_call(
        functools.partial(image_body, hops),
        grid_spec=pltpu.PrefetchScalarGridSpec(
            num_scalar_prefetch=1,
            grid=(n,),
            in_specs=in_specs,
            out_specs=[
                pl.BlockSpec((1, 2 * ROWS, WIDE), slot),
                pl.BlockSpec((1, 2 * ROWS, DH), slot),
            ],
            scratch_shapes=[
                pltpu.VMEM((VPAD, DH), jnp.bfloat16),
                pltpu.VMEM((VPAD, 2 * DH), jnp.bfloat16),
            ],
        ),
        out_shape=[PARTIAL, STATS],
        input_output_aliases=aliases,
        name="image_part",
        **params(n * 540_000_000, n * 1_400_000, n * 690_000),
    )(plan, *chunks, q, q_in, *held)


def text_scores(plan, hops, blocks, qa, qb):
    n = len(blocks)
    k = jnp.concatenate([b[:, :DH] for b in blocks], axis=0)
    v = jnp.concatenate([b[:, DH:] for b in blocks], axis=0)
    v = jnp.concatenate([v, jnp.ones_like(v)], axis=1)
    lanes = lax.broadcasted_iota(jnp.int32, (1, n * ROWS), 1)
    start = pick(lanes // ROWS, [plan[OFFSET + source(plan, hop)] for hop in hops])
    key_pos = start + lanes % ROWS
    visible = key_pos <= query_positions(plan)
    query = stack_heads(qa, qb)
    scores = lax.dot_general(
        query, k, (((1,), (1,)), ((), ())), preferred_element_type=jnp.float32
    )
    scores = scores.reshape(GROUP, 2 * ROWS, n * ROWS)
    scores = jnp.where(visible[None], scores, NEG).reshape(GROUP * 2 * ROWS, n * ROWS)
    peak = jnp.max(scores, axis=1, keepdims=True)
    weights = jnp.exp2((scores - peak) * EXP_SCALE).astype(jnp.bfloat16)
    return peak, jnp.dot(weights, v, preferred_element_type=jnp.float32)


def fold(held, stats, h, peak, summed):
    old_peak, old_total = stats[:, h : h + 1], stats[:, 8 + h : 9 + h]
    new_peak = jnp.maximum(old_peak, peak)
    old_scale = jnp.exp2((old_peak - new_peak) * EXP_SCALE)
    scale = jnp.exp2((peak - new_peak) * EXP_SCALE)
    value = old_scale * held[:, h * DH : (h + 1) * DH] + scale * summed[:, :DH]
    total = old_scale * old_total + scale * summed[:, DH:]
    return new_peak, value, total


def text_body(hops, plan, *refs):
    n = len(hops)
    blocks = [r[...] for r in refs[:n]]
    qa, qb = refs[n], refs[n + 1]
    held = refs[n + 2 : -2]
    out, stat = refs[-2:]
    peak, summed = text_scores(plan, hops, blocks, qa[0], qb[0])
    peaks, totals = [], []
    for h in range(GROUP):
        rows = slice(h * 2 * ROWS, (h + 1) * 2 * ROWS)
        if held:
            new_peak, value, total = fold(held[0][0], held[1][0], h, peak[rows], summed[rows])
        else:
            new_peak, value, total = peak[rows], summed[rows, :DH], summed[rows, DH:]
        out[0, :, h * DH : (h + 1) * DH] = value
        peaks.append(new_peak)
        totals.append(total)
    stat[0] = pack_stats(peaks, totals)


def text_part(plan, hops, chunks, q, q_in, held):
    n = len(hops)
    by_seq = lambda shape: pl.BlockSpec(shape, lambda s, plan: (s, 0, 0))
    state = [by_seq((1, 2 * ROWS, WIDE)), by_seq((1, 2 * ROWS, DH))]
    return pl.pallas_call(
        functools.partial(text_body, hops),
        grid_spec=pltpu.PrefetchScalarGridSpec(
            num_scalar_prefetch=1,
            grid=(SEQS,),
            in_specs=[pl.BlockSpec((ROWS, 2 * DH), lambda s, plan: (s, 0))] * n
            + [
                pl.BlockSpec((1, ROWS, WIDE), lambda s, plan: (s, 0, plan[X])),
                by_seq((1, ROWS, WIDE)),
            ]
            + (state if held else []),
            out_specs=state,
        ),
        out_shape=[
            jax.ShapeDtypeStruct((SEQS, 2 * ROWS, WIDE), jnp.float32),
            jax.ShapeDtypeStruct((SEQS, 2 * ROWS, DH), jnp.float32),
        ],
        name="text_part",
        **params(n * 160_000_000, 3_000_000 + n * 131_000, n * 230_000),
    )(plan, *chunks, q, q_in, *held)


def finish_body(hops, plan, *refs):
    n = len(hops)
    blocks = [r[...] for r in refs[:n]]
    qa, qb, text, text_stat = refs[n : n + 4]
    parts, part_stats = refs[n + 4 : n + 8], refs[n + 8 : n + 12]
    gates = refs[n + 12]
    mine, theirs = refs[-2:]
    peak, summed = text_scores(plan, hops, blocks, qa[0], qb[0])
    seq = pl.program_id(0)
    core = plan[SLOT + 16]
    own, other = 2 * plan[X], 2 * (1 - plan[X])
    logits = jnp.concatenate(
        [
            gates[own, 0] + gates[own + 1, 0],
            gates[other, 0] + gates[other + 1, 0],
        ],
        axis=0,
    )
    group = 2 * core + plan[X]
    logits = pick(group, [logits[:, g * GROUP : (g + 1) * GROUP] for g in range(4)])
    gate = 1.0 / (1.0 + jnp.exp(-logits))
    for h in range(GROUP):
        rows = slice(h * 2 * ROWS, (h + 1) * 2 * ROWS)
        cols = slice(h * DH, (h + 1) * DH)
        _, value, total = fold(text[0], text_stat[0], h, peak[rows], summed[rows])
        text_out = value / total
        peaks = [r[0, :, h : h + 1] for r in part_stats]
        top = functools.reduce(jnp.maximum, peaks)
        value, total = 0.0, 0.0
        for r, stats, part_peak in zip(parts, part_stats, peaks):
            scale = jnp.exp2((part_peak - top) * EXP_SCALE)
            value += scale * r[0, :, cols]
            total += scale * stats[0, :, 8 + h : 9 + h]
        visual_out = value / total
        g = gate[:, h : h + 1]
        mixed = ((1.0 - g) * text_out + g * visual_out).astype(jnp.bfloat16)
        mine[0, :, cols] = mixed[:ROWS]
        theirs[0, :, cols] = mixed[ROWS:]


def finish(plan, hops, chunks, q, q_in, text, partial, gates):
    n = len(hops)
    by_seq = lambda shape: pl.BlockSpec(shape, lambda s, plan: (s, 0, 0))
    image = lambda j, width: pl.BlockSpec(
        (1, 2 * ROWS, width), lambda s, plan, j=j: (4 * s + j, 0, 0)
    )
    mine = pl.BlockSpec((1, ROWS, WIDE), lambda s, plan: (s, 0, plan[X]))
    return pl.pallas_call(
        functools.partial(finish_body, hops),
        grid_spec=pltpu.PrefetchScalarGridSpec(
            num_scalar_prefetch=1,
            grid=(SEQS,),
            in_specs=[pl.BlockSpec((ROWS, 2 * DH), lambda s, plan: (s, 0))] * n
            + [mine, by_seq((1, ROWS, WIDE))]
            + [by_seq((1, 2 * ROWS, WIDE)), by_seq((1, 2 * ROWS, DH))]
            + [image(j, WIDE) for j in range(4)]
            + [image(j, DH) for j in range(4)]
            + [pl.BlockSpec((4, 1, ROWS, HQ), lambda s, plan: (0, s, 0, 0))],
            out_specs=[mine, by_seq((1, ROWS, WIDE))],
        ),
        out_shape=[
            jax.ShapeDtypeStruct((SEQS, ROWS, 2 * WIDE), jnp.bfloat16),
            jax.ShapeDtypeStruct((SEQS, ROWS, WIDE), jnp.bfloat16),
        ],
        name="finish",
        **params(n * 160_000_000, 12_000_000, n * 230_000),
    )(plan, *chunks, q, q_in, *text, *[partial[0]] * 4, *[partial[1]] * 4, gates)


def place_body(plan, arrived, mine, out):
    del plan, mine
    out[...] = arrived[...]


def place(plan, arrived, mine):
    shape = (SEQS, ROWS, WIDE)
    return pl.pallas_call(
        place_body,
        grid_spec=pltpu.PrefetchScalarGridSpec(
            num_scalar_prefetch=1,
            grid=(1,),
            in_specs=[
                pl.BlockSpec(shape, lambda i, plan: (0, 0, 0)),
                pl.BlockSpec(memory_space=pl.ANY),
            ],
            out_specs=pl.BlockSpec(shape, lambda i, plan: (0, 0, 1 - plan[X])),
        ),
        out_shape=jax.ShapeDtypeStruct((SEQS, ROWS, 2 * WIDE), jnp.bfloat16),
        input_output_aliases={2: 0},
        name="place",
        **params(0, 900_000, 0),
    )(plan, arrived, mine)


def on_device(
    queries,
    text_keys,
    text_values,
    visual_keys,
    visual_values,
    gate_weight,
    text_offsets,
    image_sequence,
    image_position,
):
    z, x, core = lax.axis_index("z"), lax.axis_index("x"), lax.axis_index("kvh")
    same = image_sequence[:, None] == image_sequence[None, :]
    before = jnp.arange(16)[:, None] > jnp.arange(16)[None, :]
    slot = image_sequence * 4 + jnp.sum(same & before, axis=1, dtype=jnp.int32)
    plan = jnp.concatenate(
        [
            jnp.stack([z, x]).astype(jnp.int32),
            text_offsets,
            image_sequence,
            image_position,
            slot,
            core[None].astype(jnp.int32),
        ]
    )
    swap = functools.partial(lax.ppermute, axis_name="x", perm=[(0, 1), (1, 0)])
    up = functools.partial(
        lax.ppermute, axis_name="z", perm=[(i, (i + 1) % PLANES) for i in range(PLANES)]
    )
    down = functools.partial(
        lax.ppermute, axis_name="z", perm=[(i, (i - 1) % PLANES) for i in range(PLANES)]
    )
    own, other, q_other = pack(plan, text_keys, text_values, visual_keys, visual_values, queries)
    gates = lax.all_gather(gate_share(queries, gate_weight), ("x", "kvh"), axis=0)
    got = {(0, 0): own}
    got[-1, 0], got[1, 0] = up(own), down(own)
    got[0, 1] = swap(other)
    q_in = swap(q_other)
    got[-1, 1], got[1, 1] = up(got[0, 1]), down(got[0, 1])
    for far in (2, 3):
        for stream in (0, 1):
            got[-far, stream] = up(got[1 - far, stream])
            got[far, stream] = down(got[far - 1, stream])
    got[-4, 0], got[4, 1] = up(got[-3, 0]), down(got[3, 1])

    def take(hops):
        return [got[hop] for hop in hops]

    partial = ()
    order = [[(0, 0), (0, 1)]]
    for far in (1, 2, 3):
        order += [[(-far, s), (far, s)] for s in (0, 1)]
    order += [[(-4, 0)], [(4, 1)]]
    for hops in order:
        partial = image_part(plan, hops, take(hops), queries, q_in, partial)
    first = [hop for hops in order[:5] for hop in hops]
    second = [hop for hops in order[5:7] for hop in hops]
    last = [(-4, 0), (4, 1)]
    text = text_part(plan, first, take(first), queries, q_in, ())
    text = text_part(plan, second, take(second), queries, q_in, text)
    mine, theirs = finish(plan, last, take(last), queries, q_in, text, partial, gates)
    return place(plan, swap(theirs), mine)


def solution(mesh):
    cut = Mesh(mesh.devices.reshape(PLANES, 2, 2, 8), ("z", "x", "kvh", "batch"))
    seq = ("z", "x")
    return jax.shard_map(
        on_device,
        mesh=cut,
        in_specs=(
            P("batch", seq, "kvh"),
            P("batch", seq, "kvh"),
            P("batch", seq, "kvh"),
            P(("batch",) + seq, None, "kvh"),
            P(("batch",) + seq, None, "kvh"),
            P("kvh", None),
            P("batch"),
            P("batch"),
            P("batch"),
        ),
        out_specs=P("batch", seq, "kvh"),
        check_vma=False,
    )
```

```python
import functools

import jax
import jax.numpy as jnp
from jax import lax
from jax.experimental import pallas as pl
from jax.experimental.pallas import tpu as pltpu
from jax.sharding import Mesh, PartitionSpec as P

HQ = 28
DH = 128
GROUP = 7
SEQS = 4
ROWS = 64
WIDE = GROUP * DH
VTOK = 729
VROWS = 736
VPAD = 768
TEXT = SEQS * ROWS
CHUNK = TEXT + VROWS
PLANES = 8
NEG = -1e30
EXP_SCALE = 1.4426950408889634 / DH**0.5

Z, X, CORE, OFFSET, OWNER, PLACE, SLOT = 0, 1, 2, 3, 19, 35, 51

VMEM_BYTES = 20 * 1024 * 1024
ALL_VMEM = 63 * 1024 * 1024
IMAGE_HEADS = [[0, 1], [2, 3], [4, 5], [6]]
TEXT_HEADS = [[0, 1, 2, 3], [4, 5, 6]]

TOKEN = jax.ShapeDtypeStruct((8, DH), jnp.float32)
WHOLE = pl.BlockSpec(memory_space=pltpu.VMEM)
ANYWHERE = pl.BlockSpec(memory_space=pl.ANY)


def source(plan, hop):
    plane, stream = hop
    z = lax.rem(plan[Z] + (plane + PLANES), PLANES)
    x = plan[X] if stream == 0 else 1 - plan[X]
    return 2 * z + x


def pick(step, options):
    value = options[0]
    for i in range(1, len(options)):
        value = jnp.where(step == i, options[i], value)
    return value


def params(vmem=VMEM_BYTES):
    return dict(
        compiler_params=pltpu.CompilerParams(vmem_limit_bytes=vmem),
        cost_estimate=pl.CostEstimate(flops=1000, bytes_accessed=1000, transcendentals=0),
    )


def some_heads(query, heads):
    return query[heads[0] * 2 * ROWS : (heads[-1] + 1) * 2 * ROWS]


def query_positions(plan):
    rows = lax.broadcasted_iota(jnp.int32, (2 * ROWS, 1), 0)
    own = plan[OFFSET + 2 * plan[Z] + plan[X]]
    other = plan[OFFSET + 2 * plan[Z] + 1 - plan[X]]
    return jnp.where(rows < ROWS, own + rows, other + rows - ROWS)


def pack_stats(peaks, sums):
    lanes = lax.broadcasted_iota(jnp.int32, (2 * ROWS, DH), 1)
    totals = [a[:, DH:] for a in sums]
    peak, total = peaks[0], totals[0]
    for h in range(1, GROUP):
        peak = jnp.where(lanes == h, peaks[h], peak)
        total = jnp.where(lanes == h, totals[h], total)
    return jnp.concatenate([peak, total], axis=1)


def attend(queries, k, v, limit):
    def score(query):
        return jnp.dot(query, k, preferred_element_type=jnp.float32)

    peaks, sums = [], []
    ahead = score(queries[0])
    for i in range(len(queries)):
        scores = limit(ahead)
        if i + 1 < len(queries):
            ahead = score(queries[i + 1])
        peak = jnp.max(scores, axis=1, keepdims=True)
        weights = jnp.exp2((scores - peak) * EXP_SCALE).astype(jnp.bfloat16)
        summed = jnp.dot(weights, v, preferred_element_type=jnp.float32)
        for start in range(0, scores.shape[0], 2 * ROWS):
            peaks.append(peak[start : start + 2 * ROWS])
            sums.append(summed[start : start + 2 * ROWS])
    return peaks, sums


def pack_body(tk, tv, vk, vv, q, own, other, half_q, text, visual, sems):
    x = lax.axis_index("x")
    copies = [
        pltpu.make_async_copy(src, dst, sems.at[i])
        for i, (src, dst) in enumerate(
            [
                (tk, text.at[0]),
                (tv, text.at[1]),
                (vk, visual.at[0]),
                (vv, visual.at[1]),
                (q.at[:, :, pl.ds(pl.multiple_of((1 - x) * WIDE, DH), WIDE)], half_q),
            ]
        )
    ]
    for copy in copies:
        copy.start()
    for out in (own, other):
        out[CHUNK - 16 :, :] = jnp.zeros((16, 2 * DH), jnp.bfloat16)
    for copy in copies[:4]:
        copy.wait()
    for out, group in ((other, 1 - x), (own, x)):
        cols = pl.ds(pl.multiple_of(group * DH, DH), DH)
        for i in range(2):
            half = slice(i * DH, (i + 1) * DH)
            out[:TEXT, half] = text[i, :, :, cols].reshape(TEXT, DH)
            out[TEXT : TEXT + VTOK, half] = visual[i, 0, :, cols]
    copies[4].wait()


def pack(tk, tv, vk, vv, q):
    return pl.pallas_call(
        pack_body,
        in_specs=[pl.BlockSpec(memory_space=pltpu.HBM)] * 5,
        out_specs=[WHOLE] * 3,
        out_shape=[jax.ShapeDtypeStruct((CHUNK, 2 * DH), jnp.bfloat16)] * 2
        + [jax.ShapeDtypeStruct((SEQS, ROWS, WIDE), jnp.bfloat16)],
        scratch_shapes=[
            pltpu.VMEM((2, SEQS, ROWS, 2 * DH), jnp.bfloat16),
            pltpu.VMEM((2, 1, VTOK, 2 * DH), jnp.bfloat16),
            pltpu.SemaphoreType.DMA((5,)),
        ],
        name="pack",
        **params(ALL_VMEM),
    )(tk, tv, vk, vv, q)


def split3(total):
    hi = total.astype(jnp.bfloat16)
    rest = total - hi.astype(jnp.float32)
    mid = rest.astype(jnp.bfloat16)
    return hi, mid, (rest - mid.astype(jnp.float32)).astype(jnp.bfloat16)


def share_body(q, w, _, share, token):
    token[...] = jnp.zeros_like(token)
    rows = q[...].reshape(SEQS * ROWS, 2 * WIDE)
    acc = 0.0
    for part in reversed(split3(w[...])):
        acc += lax.dot_general(
            rows, part, (((1,), (1,)), ((), ())), preferred_element_type=jnp.float32
        )
    share[...] = acc.reshape(SEQS, ROWS, HQ)


def gate_share(q, w, mark):
    return pl.pallas_call(
        share_body,
        in_specs=[WHOLE] * 2 + [ANYWHERE],
        out_specs=[WHOLE] * 2,
        out_shape=[jax.ShapeDtypeStruct((SEQS, ROWS, HQ), jnp.float32), TOKEN],
        name="gate_share",
        **params(),
    )(q, w.T, mark)


def gather_body(q_all, arrived, query, q, sem):
    cols = pl.ds(pl.multiple_of(lax.axis_index("x") * WIDE, DH), WIDE)
    copy = pltpu.make_async_copy(q_all.at[:, :, cols], q, sem)
    copy.start()
    for h in range(GROUP):
        query[:, (2 * h + 1) * ROWS : (2 * h + 2) * ROWS] = arrived[:, :, h * DH : (h + 1) * DH]
    copy.wait()
    for h in range(GROUP):
        query[:, 2 * h * ROWS : (2 * h + 1) * ROWS] = q[:, :, h * DH : (h + 1) * DH]


def gather_queries(q, arrived):
    return pl.pallas_call(
        gather_body,
        in_specs=[pl.BlockSpec(memory_space=pltpu.HBM), WHOLE],
        out_specs=WHOLE,
        out_shape=jax.ShapeDtypeStruct((SEQS, GROUP * 2 * ROWS, DH), jnp.bfloat16),
        scratch_shapes=[
            pltpu.VMEM((SEQS, ROWS, WIDE), jnp.bfloat16),
            pltpu.SemaphoreType.DMA,
        ],
        name="gather_queries",
        **params(),
    )(q, arrived)


def join(old, new, limit=DH):
    top = jnp.maximum(old[:, :limit], new[:, :limit])
    old_scale = jnp.exp2((old[:, :limit] - top) * EXP_SCALE)
    scale = jnp.exp2((new[:, :limit] - top) * EXP_SCALE)
    total = old_scale * old[:, DH : DH + limit] + scale * new[:, DH : DH + limit]
    return top, total, old_scale, scale


STATE = [
    jax.ShapeDtypeStruct((SEQS, 2 * ROWS, WIDE), jnp.float32),
    jax.ShapeDtypeStruct((SEQS, 2 * ROWS, 2 * DH), jnp.float32),
]
PARTIAL = [
    jax.ShapeDtypeStruct((4 * SEQS, 2 * ROWS, WIDE), jnp.float32),
    jax.ShapeDtypeStruct((4 * SEQS, 2 * ROWS, 2 * DH), jnp.float32),
]


def image_body(hops, plan, *refs):
    n = len(hops)
    chunks = refs[:n]
    query = refs[n]
    out, stat, token, keys, values = refs[-5:]
    token[...] = jnp.zeros_like(token)
    step = pl.program_id(0)

    @pl.when(step == 0)
    def _():
        values[:, DH:] = jnp.ones((VPAD, DH), jnp.bfloat16)
        values[VROWS:, :DH] = jnp.zeros((VPAD - VROWS, DH), jnp.bfloat16)
        keys[VROWS:, :] = jnp.zeros((VPAD - VROWS, DH), jnp.bfloat16)

    for i in range(n):

        @pl.when(step == i)
        def _(i=i):
            keys[:VROWS, :] = chunks[i][TEXT:, :DH]
            values[:VROWS, :DH] = chunks[i][TEXT:, DH:]

    place = pick(step, [plan[PLACE + source(plan, hop)] for hop in hops])
    visible = query_positions(plan) >= place
    lanes = lax.broadcasted_iota(jnp.int32, (1, DH), 1)

    def limit(scores):
        edge = jnp.where(lanes < VTOK - (VPAD - DH), scores[:, VPAD - DH :], NEG)
        return jnp.concatenate([scores[:, : VPAD - DH], edge], axis=1)

    rows = query[pick(step, [plan[OWNER + source(plan, hop)] for hop in hops])]
    queries = [some_heads(rows, heads) for heads in IMAGE_HEADS]
    peaks, sums = attend(queries, keys[...].T, values[...], limit)
    stat[0] = pack_stats([jnp.where(visible, peak, NEG) for peak in peaks], sums)
    for h in range(GROUP):
        out[0, :, h * DH : (h + 1) * DH] = sums[h][:, :DH]


TOKEN_SPEC = pl.BlockSpec((8, DH), lambda i, plan: (0, 0))


def image_part(plan, hops, chunks, query, held, mark):
    n = len(hops)

    def slot(i, plan):
        return (pick(i, [plan[SLOT + source(plan, hop)] for hop in hops]), 0, 0)

    out = pl.pallas_call(
        functools.partial(image_body, hops),
        grid_spec=pltpu.PrefetchScalarGridSpec(
            num_scalar_prefetch=1,
            grid=(n,),
            in_specs=[WHOLE] * (n + 1) + [ANYWHERE] * (1 + len(held)),
            out_specs=[pl.BlockSpec((1,) + a.shape[1:], slot) for a in PARTIAL] + [TOKEN_SPEC],
            scratch_shapes=[
                pltpu.VMEM((VPAD, DH), jnp.bfloat16),
                pltpu.VMEM((VPAD, 2 * DH), jnp.bfloat16),
            ],
        ),
        out_shape=PARTIAL + [TOKEN],
        input_output_aliases={n + 3: 0, n + 4: 1} if held else {},
        name="image_part",
        **params(),
    )(plan, *chunks, query, mark, *held)
    return out[:2], out[2]


def text_scores(plan, hops, blocks, query):
    n = len(blocks)
    k = jnp.concatenate([b[:, :DH] for b in blocks], axis=0)
    v = jnp.concatenate([b[:, DH:] for b in blocks], axis=0)
    v = jnp.concatenate([v, jnp.ones_like(v)], axis=1)
    lanes = lax.broadcasted_iota(jnp.int32, (1, n * ROWS), 1)
    start = pick(lanes // ROWS, [plan[OFFSET + source(plan, hop)] for hop in hops])
    key_pos = start + lanes % ROWS
    visible = key_pos <= query_positions(plan)
    def limit(scores):
        count = scores.shape[0] // (2 * ROWS)
        scores = scores.reshape(count, 2 * ROWS, n * ROWS)
        return jnp.where(visible[None], scores, NEG).reshape(count * 2 * ROWS, n * ROWS)

    queries = [some_heads(query, heads) for heads in TEXT_HEADS]
    return attend(queries, k.T, v, limit)


def text_body(hops, plan, *refs):
    first = 0
    n = len(hops)
    seq = pl.program_id(0) + first
    mine = pl.ds(pl.multiple_of(seq * ROWS, ROWS), ROWS)
    blocks = [r[mine, :] for r in refs[:n]]
    query = refs[n]
    held = refs[n + 2 : -3]
    out, stat, token = refs[-3:]
    token[...] = jnp.zeros_like(token)
    peaks, sums = text_scores(plan, hops, blocks, query[seq])
    stats = pack_stats(peaks, sums)
    if held:
        top, total, old_scale, scale = join(held[1][seq], stats)
        stats = jnp.concatenate([top, total], axis=1)
    stat[0] = stats
    for h in range(GROUP):
        cols = slice(h * DH, (h + 1) * DH)
        value = sums[h][:, :DH]
        if held:
            value = old_scale[:, h : h + 1] * held[0][seq, :, cols] + scale[:, h : h + 1] * value
        out[0, :, cols] = value


def text_part(plan, hops, chunks, query, held, mark):
    n = len(hops)
    by_seq = lambda shape: pl.BlockSpec(shape, lambda s, plan: (s, 0, 0))
    state = [by_seq((1,) + a.shape[1:]) for a in STATE]
    out = pl.pallas_call(
        functools.partial(text_body, hops),
        grid_spec=pltpu.PrefetchScalarGridSpec(
            num_scalar_prefetch=1,
            grid=(SEQS,),
            in_specs=[WHOLE] * (n + 1) + [ANYWHERE] + [WHOLE] * len(held),
            out_specs=state + [TOKEN_SPEC],
        ),
        out_shape=STATE + [TOKEN],
        name="text_part",
        **params(),
    )(plan, *chunks, query, mark, *held)
    return out[:2], out[2]


def finish_body(hops, first, plan, *refs):
    n = len(hops)
    seq = pl.program_id(0) + first
    mine = pl.ds(pl.multiple_of(seq * ROWS, ROWS), ROWS)
    blocks = [r[mine, :] for r in refs[:n]]
    query, text, text_stat, visual, visual_stat, gate_own, gate_in = refs[n : n + 7]
    out, theirs = refs[-2:]
    peaks, sums = text_scores(plan, hops, blocks, query[seq])
    logits = jnp.concatenate([gate_own[seq], gate_in[seq]], axis=0)
    group = 2 * plan[CORE] + plan[X]
    logits = pick(group, [logits[:, g * GROUP : (g + 1) * GROUP] for g in range(4)])
    gate = 1.0 / (1.0 + jnp.exp(-logits))
    _, total, old_scale, scale = join(text_stat[seq], pack_stats(peaks, sums), GROUP)
    text_factor = (1.0 - gate) / total
    places = [4 * seq + j for j in range(4)]
    tops = [visual_stat[place, :, :GROUP] for place in places]
    top = functools.reduce(jnp.maximum, tops)
    scales = [jnp.exp2((a - top) * EXP_SCALE) for a in tops]
    totals = [a * visual_stat[i, :, DH : DH + GROUP] for a, i in zip(scales, places)]
    visual_factor = gate / sum(totals)
    factors = [text_factor * scale, text_factor * old_scale]
    factors += [visual_factor * a for a in scales]
    for h in range(GROUP):
        cols = slice(h * DH, (h + 1) * DH)
        values = [sums[h][:, :DH], text[seq, :, cols]] + [visual[i, :, cols] for i in places]
        mixed = sum(factor[:, h : h + 1] * value for factor, value in zip(factors, values))
        mixed = mixed.astype(jnp.bfloat16)
        out[0, :, cols] = mixed[:ROWS]
        theirs[0, :, cols] = mixed[ROWS:]


def finish(plan, hops, seqs, chunks, query, text, visual, gates, held):
    n, first, count = len(hops), seqs[0], len(seqs)
    mine = pl.BlockSpec((1, ROWS, WIDE), lambda s, plan: (first + s, 0, plan[X]))
    return pl.pallas_call(
        functools.partial(finish_body, hops, seqs[0]),
        grid_spec=pltpu.PrefetchScalarGridSpec(
            num_scalar_prefetch=1,
            grid=(count,),
            in_specs=[WHOLE] * (n + 7) + [ANYWHERE] * len(held),
            out_specs=[mine, pl.BlockSpec((1, ROWS, WIDE), lambda s, plan: (s, 0, 0))],
        ),
        out_shape=[
            jax.ShapeDtypeStruct((SEQS, ROWS, 2 * WIDE), jnp.bfloat16),
            jax.ShapeDtypeStruct((count, ROWS, WIDE), jnp.bfloat16),
        ],
        input_output_aliases={n + 8: 0} if held else {},
        name="finish",
        **params(),
    )(plan, *chunks, query, *text, *visual, *gates, *held)


def place_body(plan, arrived, mine, out):
    del plan, mine
    out[...] = arrived[...]


def place(plan, seqs, arrived, mine):
    shape = (len(seqs), ROWS, WIDE)
    block = seqs[0] // len(seqs)
    return pl.pallas_call(
        place_body,
        grid_spec=pltpu.PrefetchScalarGridSpec(
            num_scalar_prefetch=1,
            grid=(1,),
            in_specs=[
                pl.BlockSpec(shape, lambda i, plan: (0, 0, 0)),
                pl.BlockSpec(memory_space=pl.ANY),
            ],
            out_specs=pl.BlockSpec(shape, lambda i, plan: (block, 0, 1 - plan[X])),
        ),
        out_shape=jax.ShapeDtypeStruct((SEQS, ROWS, 2 * WIDE), jnp.bfloat16),
        input_output_aliases={2: 0},
        name="place",
        **params(),
    )(plan, arrived, mine)


def on_device(
    queries,
    text_keys,
    text_values,
    visual_keys,
    visual_values,
    gate_weight,
    text_offsets,
    image_sequence,
    image_position,
):
    z, x, core = lax.axis_index("z"), lax.axis_index("x"), lax.axis_index("kvh")
    same = image_sequence[:, None] == image_sequence[None, :]
    before = jnp.arange(16)[:, None] > jnp.arange(16)[None, :]
    slot = image_sequence * 4 + jnp.sum(same & before, axis=1, dtype=jnp.int32)
    plan = jnp.concatenate(
        [
            jnp.stack([z, x, core]).astype(jnp.int32),
            text_offsets,
            image_sequence,
            image_position,
            slot,
        ]
    )
    swap = functools.partial(lax.ppermute, axis_name="x", perm=[(0, 1), (1, 0)])
    up = functools.partial(
        lax.ppermute, axis_name="z", perm=[(i, (i + 1) % PLANES) for i in range(PLANES)]
    )
    down = functools.partial(
        lax.ppermute, axis_name="z", perm=[(i, (i - 1) % PLANES) for i in range(PLANES)]
    )
    tie = lax.optimization_barrier
    own, other, half_q = pack(text_keys, text_values, visual_keys, visual_values, queries)
    got = {(0, 0): own}
    visual = ()
    text = ()

    def take(hops):
        return [got[hop] for hop in hops]

    mark = None

    def images(*hops):
        nonlocal visual, mark
        visual, mark = image_part(plan, list(hops), take(hops), query, visual, mark)

    def texts(*hops):
        nonlocal text, mark
        text, mark = text_part(plan, list(hops), take(hops), query, text, mark)

    def relay(plane, stream):
        nonlocal mark
        back, front = got[1 - plane, stream], got[plane - 1, stream]
        if mark is not None:
            back, front, mark = tie((back, front, mark))
        if plane < 4 or stream == 0:
            got[-plane, stream] = up(back)
        if plane < 4 or stream == 1:
            got[plane, stream] = down(front)

    relay(1, 0)
    got[0, 1] = swap(other)
    arrived = swap(half_q)
    relay(1, 1)
    query = gather_queries(queries, arrived)
    relay(2, 0)
    mark = query
    images((0, 0), (0, 1))
    images((-1, 0), (1, 0))
    relay(2, 1)
    share, mark = gate_share(queries, gate_weight, mark)
    logits = share + lax.ppermute(share, "kvh", [(0, 1), (1, 0)])
    images((-1, 1), (1, 1))
    relay(3, 0)
    images((-2, 0), (2, 0))
    mark, logits = tie((mark, logits))
    gates = (logits, swap(logits))
    texts((0, 0), (0, 1), (-1, 0), (1, 0), (-1, 1), (1, 1))
    relay(3, 1)
    images((-2, 1), (2, 1))
    relay(4, 0)
    images((-3, 0), (3, 0))
    texts((-2, 0), (2, 0), (-2, 1), (2, 1), (-3, 0), (3, 0))
    relay(4, 1)
    images((-3, 1), (3, 1))
    texts((-3, 1), (3, 1))
    images((-4, 0),)
    images((4, 1),)
    last = [(-4, 0), (4, 1)]
    state = (take(last), query, text, visual, gates)
    mine, theirs = finish(plan, last, (0, 1), *state, ())
    arrived = swap(theirs)
    mine, theirs = finish(plan, last, (2, 3), *state, (mine,))
    arrived_next = swap(theirs)
    mine = place(plan, (0, 1), arrived, mine)
    return place(plan, (2, 3), arrived_next, mine)


def solution(mesh):
    cut = Mesh(mesh.devices.reshape(PLANES, 2, 2, 8), ("z", "x", "kvh", "batch"))
    seq = ("z", "x")
    return jax.shard_map(
        on_device,
        mesh=cut,
        in_specs=(
            P("batch", seq, "kvh"),
            P("batch", seq, "kvh"),
            P("batch", seq, "kvh"),
            P(("batch",) + seq, None, "kvh"),
            P(("batch",) + seq, None, "kvh"),
            P("kvh", None),
            P("batch"),
            P("batch"),
            P("batch"),
        ),
        out_specs=P("batch", seq, "kvh"),
        check_vma=False,
    )
```

```python
import functools

import jax
import jax.numpy as jnp
from jax import lax
from jax.experimental import pallas as pl
from jax.experimental.pallas import tpu as pltpu
from jax.sharding import Mesh, PartitionSpec as P

HQ = 28
DH = 128
GROUP = 7
SEQS = 4
ROWS = 64
WIDE = GROUP * DH
VTOK = 729
VROWS = 736
VPAD = 768
TEXT = SEQS * ROWS
CHUNK = TEXT + VROWS
PLANES = 8
NEG = -1e30
EXP_SCALE = 1.4426950408889634 / DH**0.5

Z, X, CORE, OFFSET, OWNER, PLACE, SLOT = 0, 1, 2, 3, 19, 35, 51

VMEM_BYTES = 20 * 1024 * 1024
ALL_VMEM = 63 * 1024 * 1024
IMAGE_HEADS = [[0, 1], [2, 3], [4, 5], [6]]
TEXT_HEADS = [[0, 1, 2, 3], [4, 5, 6]]

TOKEN = jax.ShapeDtypeStruct((8, DH), jnp.float32)
WHOLE = pl.BlockSpec(memory_space=pltpu.VMEM)
ANYWHERE = pl.BlockSpec(memory_space=pl.ANY)


def source(plan, hop):
    plane, stream = hop
    z = lax.rem(plan[Z] + (plane + PLANES), PLANES)
    x = plan[X] if stream == 0 else 1 - plan[X]
    return 2 * z + x


def pick(step, options):
    value = options[0]
    for i in range(1, len(options)):
        value = jnp.where(step == i, options[i], value)
    return value


def params(vmem=VMEM_BYTES):
    return dict(
        compiler_params=pltpu.CompilerParams(vmem_limit_bytes=vmem),
        cost_estimate=pl.CostEstimate(flops=1000, bytes_accessed=1000, transcendentals=0),
    )


def some_heads(query, heads):
    return query[heads[0] * 2 * ROWS : (heads[-1] + 1) * 2 * ROWS]


def query_positions(plan):
    rows = lax.broadcasted_iota(jnp.int32, (2 * ROWS, 1), 0)
    own = plan[OFFSET + 2 * plan[Z] + plan[X]]
    other = plan[OFFSET + 2 * plan[Z] + 1 - plan[X]]
    return jnp.where(rows < ROWS, own + rows, other + rows - ROWS)


def pack_stats(peaks, sums):
    lanes = lax.broadcasted_iota(jnp.int32, (2 * ROWS, DH), 1)
    totals = [a[:, DH:] for a in sums]
    peak, total = peaks[0], totals[0]
    for h in range(1, GROUP):
        peak = jnp.where(lanes == h, peaks[h], peak)
        total = jnp.where(lanes == h, totals[h], total)
    return jnp.concatenate([peak, total], axis=1)


def attend(jobs, limit):
    def score(job):
        return jnp.dot(job[0], job[1], preferred_element_type=jnp.float32)

    peaks, sums = [], []
    ahead = score(jobs[0])
    for i, job in enumerate(jobs):
        scores = limit(ahead)
        if i + 1 < len(jobs):
            ahead = score(jobs[i + 1])
        peak = jnp.max(scores, axis=1, keepdims=True)
        weights = jnp.exp2((scores - peak) * EXP_SCALE).astype(jnp.bfloat16)
        summed = jnp.dot(weights, job[2], preferred_element_type=jnp.float32)
        for start in range(0, scores.shape[0], 2 * ROWS):
            peaks.append(peak[start : start + 2 * ROWS])
            sums.append(summed[start : start + 2 * ROWS])
    return peaks, sums


def pack_body(tk, tv, vk, vv, q, own, other, half_q, text, visual, sems):
    x = lax.axis_index("x")
    copies = [
        pltpu.make_async_copy(src, dst, sems.at[i])
        for i, (src, dst) in enumerate(
            [
                (tk, text.at[0]),
                (tv, text.at[1]),
                (vk, visual.at[0]),
                (vv, visual.at[1]),
                (q.at[:, :, pl.ds(pl.multiple_of((1 - x) * WIDE, DH), WIDE)], half_q),
            ]
        )
    ]
    for copy in copies:
        copy.start()
    for out in (own, other):
        out[CHUNK - 16 :, :] = jnp.zeros((16, 2 * DH), jnp.bfloat16)
    for copy in copies[:4]:
        copy.wait()
    for out, group in ((other, 1 - x), (own, x)):
        cols = pl.ds(pl.multiple_of(group * DH, DH), DH)
        for i in range(2):
            half = slice(i * DH, (i + 1) * DH)
            out[:TEXT, half] = text[i, :, :, cols].reshape(TEXT, DH)
            out[TEXT : TEXT + VTOK, half] = visual[i, 0, :, cols]
    copies[4].wait()


def pack(tk, tv, vk, vv, q):
    return pl.pallas_call(
        pack_body,
        in_specs=[pl.BlockSpec(memory_space=pltpu.HBM)] * 5,
        out_specs=[WHOLE] * 3,
        out_shape=[jax.ShapeDtypeStruct((CHUNK, 2 * DH), jnp.bfloat16)] * 2
        + [jax.ShapeDtypeStruct((SEQS, ROWS, WIDE), jnp.bfloat16)],
        scratch_shapes=[
            pltpu.VMEM((2, SEQS, ROWS, 2 * DH), jnp.bfloat16),
            pltpu.VMEM((2, 1, VTOK, 2 * DH), jnp.bfloat16),
            pltpu.SemaphoreType.DMA((5,)),
        ],
        name="pack",
        **params(ALL_VMEM),
    )(tk, tv, vk, vv, q)


def split3(total):
    hi = total.astype(jnp.bfloat16)
    rest = total - hi.astype(jnp.float32)
    mid = rest.astype(jnp.bfloat16)
    return hi, mid, (rest - mid.astype(jnp.float32)).astype(jnp.bfloat16)


def share_body(q, w, _, share, token):
    token[...] = jnp.zeros_like(token)
    rows = q[...].reshape(SEQS * ROWS, 2 * WIDE)
    acc = 0.0
    for part in reversed(split3(w[...])):
        acc += lax.dot_general(
            rows, part, (((1,), (1,)), ((), ())), preferred_element_type=jnp.float32
        )
    share[...] = acc.reshape(SEQS, ROWS, HQ)


def gate_share(q, w, mark):
    return pl.pallas_call(
        share_body,
        in_specs=[WHOLE] * 2 + [ANYWHERE],
        out_specs=[WHOLE] * 2,
        out_shape=[jax.ShapeDtypeStruct((SEQS, ROWS, HQ), jnp.float32), TOKEN],
        name="gate_share",
        **params(),
    )(q, w.T, mark)


def gather_body(q_all, arrived, query, q, sem):
    cols = pl.ds(pl.multiple_of(lax.axis_index("x") * WIDE, DH), WIDE)
    copy = pltpu.make_async_copy(q_all.at[:, :, cols], q, sem)
    copy.start()
    for h in range(GROUP):
        query[:, (2 * h + 1) * ROWS : (2 * h + 2) * ROWS] = arrived[:, :, h * DH : (h + 1) * DH]
    copy.wait()
    for h in range(GROUP):
        query[:, 2 * h * ROWS : (2 * h + 1) * ROWS] = q[:, :, h * DH : (h + 1) * DH]


def gather_queries(q, arrived):
    return pl.pallas_call(
        gather_body,
        in_specs=[pl.BlockSpec(memory_space=pltpu.HBM), WHOLE],
        out_specs=WHOLE,
        out_shape=jax.ShapeDtypeStruct((SEQS, GROUP * 2 * ROWS, DH), jnp.bfloat16),
        scratch_shapes=[
            pltpu.VMEM((SEQS, ROWS, WIDE), jnp.bfloat16),
            pltpu.SemaphoreType.DMA,
        ],
        name="gather_queries",
        **params(),
    )(q, arrived)


def join(old, new, limit=DH):
    top = jnp.maximum(old[:, :limit], new[:, :limit])
    old_scale = jnp.exp2((old[:, :limit] - top) * EXP_SCALE)
    scale = jnp.exp2((new[:, :limit] - top) * EXP_SCALE)
    total = old_scale * old[:, DH : DH + limit] + scale * new[:, DH : DH + limit]
    return top, total, old_scale, scale


STATE = [
    jax.ShapeDtypeStruct((SEQS, 2 * ROWS, WIDE), jnp.float32),
    jax.ShapeDtypeStruct((SEQS, 2 * ROWS, 2 * DH), jnp.float32),
]
PARTIAL = [
    jax.ShapeDtypeStruct((4 * SEQS, 2 * ROWS, WIDE), jnp.float32),
    jax.ShapeDtypeStruct((4 * SEQS, 2 * ROWS, 2 * DH), jnp.float32),
]


def image_body(hops, plan, *refs):
    n = len(hops)
    chunks = refs[:n]
    query = refs[n]
    out, stat, token, keys, values = refs[-5:]
    token[...] = jnp.zeros_like(token)
    step = pl.program_id(0)

    @pl.when(step == 0)
    def _():
        values[:, DH:] = jnp.ones((VPAD, DH), jnp.bfloat16)
        values[VROWS:, :DH] = jnp.zeros((VPAD - VROWS, DH), jnp.bfloat16)
        keys[VROWS:, :] = jnp.zeros((VPAD - VROWS, DH), jnp.bfloat16)

    for i in range(n):

        @pl.when(step == i)
        def _(i=i):
            keys[:VROWS, :] = chunks[i][TEXT:, :DH]
            values[:VROWS, :DH] = chunks[i][TEXT:, DH:]

    place = pick(step, [plan[PLACE + source(plan, hop)] for hop in hops])
    visible = query_positions(plan) >= place
    lanes = lax.broadcasted_iota(jnp.int32, (1, DH), 1)

    def limit(scores):
        edge = jnp.where(lanes < VTOK - (VPAD - DH), scores[:, VPAD - DH :], NEG)
        return jnp.concatenate([scores[:, : VPAD - DH], edge], axis=1)

    rows = query[pick(step, [plan[OWNER + source(plan, hop)] for hop in hops])]
    k, v = keys[...].T, values[...]
    peaks, sums = attend([(some_heads(rows, heads), k, v) for heads in IMAGE_HEADS], limit)
    stat[0] = pack_stats([jnp.where(visible, peak, NEG) for peak in peaks], sums)
    for h in range(GROUP):
        out[0, :, h * DH : (h + 1) * DH] = sums[h][:, :DH]


TOKEN_SPEC = pl.BlockSpec((8, DH), lambda i, plan: (0, 0))


def image_part(plan, hops, chunks, query, held, mark):
    n = len(hops)

    def slot(i, plan):
        return (pick(i, [plan[SLOT + source(plan, hop)] for hop in hops]), 0, 0)

    out = pl.pallas_call(
        functools.partial(image_body, hops),
        grid_spec=pltpu.PrefetchScalarGridSpec(
            num_scalar_prefetch=1,
            grid=(n,),
            in_specs=[WHOLE] * (n + 1) + [ANYWHERE] * (1 + len(held)),
            out_specs=[pl.BlockSpec((1,) + a.shape[1:], slot) for a in PARTIAL] + [TOKEN_SPEC],
            scratch_shapes=[
                pltpu.VMEM((VPAD, DH), jnp.bfloat16),
                pltpu.VMEM((VPAD, 2 * DH), jnp.bfloat16),
            ],
        ),
        out_shape=PARTIAL + [TOKEN],
        input_output_aliases={n + 3: 0, n + 4: 1} if held else {},
        name="image_part",
        **params(),
    )(plan, *chunks, query, mark, *held)
    return out[:2], out[2]


def text_scores(plan, hops, chunks, query, seqs):
    n = len(hops)
    lanes = lax.broadcasted_iota(jnp.int32, (1, n * ROWS), 1)
    start = pick(lanes // ROWS, [plan[OFFSET + source(plan, hop)] for hop in hops])
    key_pos = start + lanes % ROWS
    visible = key_pos <= query_positions(plan)
    jobs = []
    for seq in seqs:
        mine = slice(seq * ROWS, (seq + 1) * ROWS)
        k = jnp.concatenate([r[mine, :DH] for r in chunks], axis=0).T
        v = jnp.concatenate([r[mine, DH:] for r in chunks], axis=0)
        v = jnp.concatenate([v, jnp.ones_like(v)], axis=1)
        jobs += [(some_heads(query[seq], heads), k, v) for heads in TEXT_HEADS]

    def limit(scores):
        count = scores.shape[0] // (2 * ROWS)
        scores = scores.reshape(count, 2 * ROWS, n * ROWS)
        return jnp.where(visible[None], scores, NEG).reshape(count * 2 * ROWS, n * ROWS)

    peaks, sums = attend(jobs, limit)
    cut = [slice(i * GROUP, (i + 1) * GROUP) for i in range(len(seqs))]
    return [(peaks[c], sums[c]) for c in cut]


def text_body(hops, plan, *refs):
    n = len(hops)
    held = refs[n + 2 : -3]
    out, stat, token = refs[-3:]
    token[...] = jnp.zeros_like(token)
    for seq, (peaks, sums) in enumerate(
        text_scores(plan, hops, refs[:n], refs[n], range(SEQS))
    ):
        stats = pack_stats(peaks, sums)
        if held:
            top, total, old_scale, scale = join(held[1][seq], stats)
            stats = jnp.concatenate([top, total], axis=1)
        stat[seq] = stats
        for h in range(GROUP):
            cols = slice(h * DH, (h + 1) * DH)
            value = sums[h][:, :DH]
            if held:
                value = old_scale[:, h : h + 1] * held[0][seq, :, cols] + scale[:, h : h + 1] * value
            out[seq, :, cols] = value


def text_part(plan, hops, chunks, query, held, mark):
    n = len(hops)
    out = pl.pallas_call(
        functools.partial(text_body, hops),
        grid_spec=pltpu.PrefetchScalarGridSpec(
            num_scalar_prefetch=1,
            grid=(1,),
            in_specs=[WHOLE] * (n + 1) + [ANYWHERE] + [WHOLE] * len(held),
            out_specs=[WHOLE] * 3,
        ),
        out_shape=STATE + [TOKEN],
        name="text_part",
        **params(),
    )(plan, *chunks, query, mark, *held)
    return out[:2], out[2]


def finish_body(hops, seqs, plan, *refs):
    n = len(hops)
    query, text, text_stat, visual, visual_stat, gate_own, gate_in = refs[n : n + 7]
    out, theirs = refs[-2:]
    group = 2 * plan[CORE] + plan[X]
    scored = text_scores(plan, hops, refs[:n], query, seqs)
    for row, (seq, (peaks, sums)) in enumerate(zip(seqs, scored)):
        logits = jnp.concatenate([gate_own[seq], gate_in[seq]], axis=0)
        logits = pick(group, [logits[:, g * GROUP : (g + 1) * GROUP] for g in range(4)])
        gate = 1.0 / (1.0 + jnp.exp(-logits))
        _, total, old_scale, scale = join(text_stat[seq], pack_stats(peaks, sums), GROUP)
        text_factor = (1.0 - gate) / total
        places = [4 * seq + j for j in range(4)]
        tops = [visual_stat[place, :, :GROUP] for place in places]
        top = functools.reduce(jnp.maximum, tops)
        scales = [jnp.exp2((a - top) * EXP_SCALE) for a in tops]
        totals = [a * visual_stat[i, :, DH : DH + GROUP] for a, i in zip(scales, places)]
        visual_factor = gate / sum(totals)
        factors = [text_factor * scale, text_factor * old_scale]
        factors += [visual_factor * a for a in scales]
        for h in range(GROUP):
            cols = slice(h * DH, (h + 1) * DH)
            values = [sums[h][:, :DH], text[seq, :, cols]] + [visual[i, :, cols] for i in places]
            mixed = sum(factor[:, h : h + 1] * value for factor, value in zip(factors, values))
            mixed = mixed.astype(jnp.bfloat16)
            out[row, :, cols] = mixed[:ROWS]
            theirs[row, :, cols] = mixed[ROWS:]


def finish(plan, hops, seqs, chunks, query, text, visual, gates, held):
    n, count = len(hops), len(seqs)
    block = seqs[0] // count
    mine = pl.BlockSpec((count, ROWS, WIDE), lambda i, plan: (block, 0, plan[X]))
    return pl.pallas_call(
        functools.partial(finish_body, hops, seqs),
        grid_spec=pltpu.PrefetchScalarGridSpec(
            num_scalar_prefetch=1,
            grid=(1,),
            in_specs=[WHOLE] * (n + 7) + [ANYWHERE] * len(held),
            out_specs=[mine, WHOLE],
        ),
        out_shape=[
            jax.ShapeDtypeStruct((SEQS, ROWS, 2 * WIDE), jnp.bfloat16),
            jax.ShapeDtypeStruct((count, ROWS, WIDE), jnp.bfloat16),
        ],
        input_output_aliases={n + 8: 0} if held else {},
        name="finish",
        **params(),
    )(plan, *chunks, query, *text, *visual, *gates, *held)


def place_body(plan, arrived, mine, out):
    del plan, mine
    out[...] = arrived[...]


def place(plan, seqs, arrived, mine):
    shape = (len(seqs), ROWS, WIDE)
    block = seqs[0] // len(seqs)
    return pl.pallas_call(
        place_body,
        grid_spec=pltpu.PrefetchScalarGridSpec(
            num_scalar_prefetch=1,
            grid=(1,),
            in_specs=[
                pl.BlockSpec(shape, lambda i, plan: (0, 0, 0)),
                pl.BlockSpec(memory_space=pl.ANY),
            ],
            out_specs=pl.BlockSpec(shape, lambda i, plan: (block, 0, 1 - plan[X])),
        ),
        out_shape=jax.ShapeDtypeStruct((SEQS, ROWS, 2 * WIDE), jnp.bfloat16),
        input_output_aliases={2: 0},
        name="place",
        **params(),
    )(plan, arrived, mine)


def on_device(
    queries,
    text_keys,
    text_values,
    visual_keys,
    visual_values,
    gate_weight,
    text_offsets,
    image_sequence,
    image_position,
):
    z, x, core = lax.axis_index("z"), lax.axis_index("x"), lax.axis_index("kvh")
    same = image_sequence[:, None] == image_sequence[None, :]
    before = jnp.arange(16)[:, None] > jnp.arange(16)[None, :]
    slot = image_sequence * 4 + jnp.sum(same & before, axis=1, dtype=jnp.int32)
    plan = jnp.concatenate(
        [
            jnp.stack([z, x, core]).astype(jnp.int32),
            text_offsets,
            image_sequence,
            image_position,
            slot,
        ]
    )
    swap = functools.partial(lax.ppermute, axis_name="x", perm=[(0, 1), (1, 0)])
    up = functools.partial(
        lax.ppermute, axis_name="z", perm=[(i, (i + 1) % PLANES) for i in range(PLANES)]
    )
    down = functools.partial(
        lax.ppermute, axis_name="z", perm=[(i, (i - 1) % PLANES) for i in range(PLANES)]
    )
    tie = lax.optimization_barrier
    own, other, half_q = pack(text_keys, text_values, visual_keys, visual_values, queries)
    got = {(0, 0): own}
    visual = ()
    text = ()

    def take(hops):
        return [got[hop] for hop in hops]

    mark = None

    def images(*hops):
        nonlocal visual, mark
        visual, mark = image_part(plan, list(hops), take(hops), query, visual, mark)

    def texts(*hops):
        nonlocal text, mark
        text, mark = text_part(plan, list(hops), take(hops), query, text, mark)

    def relay(plane, stream):
        nonlocal mark
        back, front = got[1 - plane, stream], got[plane - 1, stream]
        if mark is not None:
            back, front, mark = tie((back, front, mark))
        if plane < 4 or stream == 0:
            got[-plane, stream] = up(back)
        if plane < 4 or stream == 1:
            got[plane, stream] = down(front)

    relay(1, 0)
    got[0, 1] = swap(other)
    arrived = swap(half_q)
    relay(1, 1)
    query = gather_queries(queries, arrived)
    relay(2, 0)
    mark = query
    images((0, 0), (0, 1))
    relay(2, 1)
    images((-1, 0), (1, 0))
    share, mark = gate_share(queries, gate_weight, mark)
    logits = share + lax.ppermute(share, "kvh", [(0, 1), (1, 0)])
    relay(3, 0)
    images((-1, 1), (1, 1))
    images((-2, 0), (2, 0))
    relay(3, 1)
    mark, logits = tie((mark, logits))
    gates = (logits, swap(logits))
    images((-2, 1), (2, 1))
    texts((0, 0), (0, 1), (-1, 0), (1, 0), (-1, 1), (1, 1))
    relay(4, 0)
    images((-3, 0), (3, 0))
    relay(4, 1)
    images((-3, 1), (3, 1))
    texts((-2, 0), (2, 0), (-2, 1), (2, 1), (-3, 0), (3, 0), (-3, 1), (3, 1))
    images((-4, 0),)
    images((4, 1),)
    last = [(-4, 0), (4, 1)]
    state = (take(last), query, text, visual, gates)
    mine, theirs = finish(plan, last, (0, 1), *state, ())
    arrived = swap(theirs)
    mine, theirs = finish(plan, last, (2, 3), *state, (mine,))
    arrived_next = swap(theirs)
    mine = place(plan, (0, 1), arrived, mine)
    return place(plan, (2, 3), arrived_next, mine)


def solution(mesh):
    cut = Mesh(mesh.devices.reshape(PLANES, 2, 2, 8), ("z", "x", "kvh", "batch"))
    seq = ("z", "x")
    return jax.shard_map(
        on_device,
        mesh=cut,
        in_specs=(
            P("batch", seq, "kvh"),
            P("batch", seq, "kvh"),
            P("batch", seq, "kvh"),
            P(("batch",) + seq, None, "kvh"),
            P(("batch",) + seq, None, "kvh"),
            P("kvh", None),
            P("batch"),
            P("batch"),
            P("batch"),
        ),
        out_specs=P("batch", seq, "kvh"),
        check_vma=False,
    )
```

```python
import functools

import jax
import jax.numpy as jnp
from jax import lax
from jax.experimental import pallas as pl
from jax.experimental.pallas import tpu as pltpu
from jax.sharding import Mesh, PartitionSpec as P

HQ = 28
DH = 128
GROUP = 7
SEQS = 4
ROWS = 64
WIDE = GROUP * DH
VTOK = 729
VROWS = 736
VPAD = 768
TEXT = SEQS * ROWS
CHUNK = TEXT + VROWS
PLANES = 8
NEG = -1e30
EXP_SCALE = 1.4426950408889634 / DH**0.5

Z, X, CORE, OFFSET, OWNER, PLACE, SLOT = 0, 1, 2, 3, 19, 35, 51

VMEM_BYTES = 20 * 1024 * 1024
ALL_VMEM = 63 * 1024 * 1024
IMAGE_HEADS = [[0, 1], [2, 3], [4, 5], [6]]
TEXT_HEADS = [[0, 1, 2, 3], [4, 5, 6]]

TOKEN = jax.ShapeDtypeStruct((8, DH), jnp.float32)
WHOLE = pl.BlockSpec(memory_space=pltpu.VMEM)
ANYWHERE = pl.BlockSpec(memory_space=pl.ANY)


def source(plan, hop):
    plane, stream = hop
    z = lax.rem(plan[Z] + (plane + PLANES), PLANES)
    x = plan[X] if stream == 0 else 1 - plan[X]
    return 2 * z + x


def pick(step, options):
    value = options[0]
    for i in range(1, len(options)):
        value = jnp.where(step == i, options[i], value)
    return value


def params(vmem=VMEM_BYTES):
    return dict(
        compiler_params=pltpu.CompilerParams(vmem_limit_bytes=vmem),
        cost_estimate=pl.CostEstimate(flops=1000, bytes_accessed=1000, transcendentals=0),
    )


def some_heads(query, heads):
    return query[heads[0] * 2 * ROWS : (heads[-1] + 1) * 2 * ROWS]


def query_positions(plan):
    rows = lax.broadcasted_iota(jnp.int32, (2 * ROWS, 1), 0)
    own = plan[OFFSET + 2 * plan[Z] + plan[X]]
    other = plan[OFFSET + 2 * plan[Z] + 1 - plan[X]]
    return jnp.where(rows < ROWS, own + rows, other + rows - ROWS)


def pack_stats(peaks, sums):
    lanes = lax.broadcasted_iota(jnp.int32, (2 * ROWS, DH), 1)
    totals = [a[:, DH:] for a in sums]
    peak, total = peaks[0], totals[0]
    for h in range(1, GROUP):
        peak = jnp.where(lanes == h, peaks[h], peak)
        total = jnp.where(lanes == h, totals[h], total)
    return jnp.concatenate([peak, total], axis=1)


def attend(jobs, limit):
    def score(job):
        return jnp.dot(job[0], job[1], preferred_element_type=jnp.float32)

    peaks, sums = [], []
    ahead = score(jobs[0])
    for i, job in enumerate(jobs):
        scores = limit(ahead)
        if i + 1 < len(jobs):
            ahead = score(jobs[i + 1])
        peak = jnp.max(scores, axis=1, keepdims=True)
        weights = jnp.exp2((scores - peak) * EXP_SCALE).astype(jnp.bfloat16)
        summed = jnp.dot(weights, job[2], preferred_element_type=jnp.float32)
        for start in range(0, scores.shape[0], 2 * ROWS):
            peaks.append(peak[start : start + 2 * ROWS])
            sums.append(summed[start : start + 2 * ROWS])
    return peaks, sums


def pack_body(tk, tv, vk, vv, q, own, other, half_q, text, visual, sems):
    x = lax.axis_index("x")
    copies = [
        pltpu.make_async_copy(src, dst, sems.at[i])
        for i, (src, dst) in enumerate(
            [
                (tk, text.at[0]),
                (tv, text.at[1]),
                (vk, visual.at[0]),
                (vv, visual.at[1]),
                (q.at[:, :, pl.ds(pl.multiple_of((1 - x) * WIDE, DH), WIDE)], half_q),
            ]
        )
    ]
    for copy in copies:
        copy.start()
    for out in (own, other):
        out[CHUNK - 16 :, :] = jnp.zeros((16, 2 * DH), jnp.bfloat16)
    for copy in copies[:4]:
        copy.wait()
    for out, group in ((other, 1 - x), (own, x)):
        cols = pl.ds(pl.multiple_of(group * DH, DH), DH)
        for i in range(2):
            half = slice(i * DH, (i + 1) * DH)
            out[:TEXT, half] = text[i, :, :, cols].reshape(TEXT, DH)
            out[TEXT : TEXT + VTOK, half] = visual[i, 0, :, cols]
    copies[4].wait()


def pack(tk, tv, vk, vv, q):
    return pl.pallas_call(
        pack_body,
        in_specs=[pl.BlockSpec(memory_space=pltpu.HBM)] * 5,
        out_specs=[WHOLE] * 3,
        out_shape=[jax.ShapeDtypeStruct((CHUNK, 2 * DH), jnp.bfloat16)] * 2
        + [jax.ShapeDtypeStruct((SEQS, ROWS, WIDE), jnp.bfloat16)],
        scratch_shapes=[
            pltpu.VMEM((2, SEQS, ROWS, 2 * DH), jnp.bfloat16),
            pltpu.VMEM((2, 1, VTOK, 2 * DH), jnp.bfloat16),
            pltpu.SemaphoreType.DMA((5,)),
        ],
        name="pack",
        **params(ALL_VMEM),
    )(tk, tv, vk, vv, q)


def split3(total):
    hi = total.astype(jnp.bfloat16)
    rest = total - hi.astype(jnp.float32)
    mid = rest.astype(jnp.bfloat16)
    return hi, mid, (rest - mid.astype(jnp.float32)).astype(jnp.bfloat16)


def share_body(q, w, _, share, token):
    token[...] = jnp.zeros_like(token)
    rows = q[...].reshape(SEQS * ROWS, 2 * WIDE)
    acc = 0.0
    for part in reversed(split3(w[...])):
        acc += lax.dot_general(
            rows, part, (((1,), (1,)), ((), ())), preferred_element_type=jnp.float32
        )
    share[...] = acc.reshape(SEQS, ROWS, HQ)


def gate_share(q, w, mark):
    return pl.pallas_call(
        share_body,
        in_specs=[WHOLE] * 2 + [ANYWHERE],
        out_specs=[WHOLE] * 2,
        out_shape=[jax.ShapeDtypeStruct((SEQS, ROWS, HQ), jnp.float32), TOKEN],
        name="gate_share",
        **params(),
    )(q, w.T, mark)


def gather_body(q_all, arrived, query, q, sem):
    cols = pl.ds(pl.multiple_of(lax.axis_index("x") * WIDE, DH), WIDE)
    copy = pltpu.make_async_copy(q_all.at[:, :, cols], q, sem)
    copy.start()
    for h in range(GROUP):
        query[:, (2 * h + 1) * ROWS : (2 * h + 2) * ROWS] = arrived[:, :, h * DH : (h + 1) * DH]
    copy.wait()
    for h in range(GROUP):
        query[:, 2 * h * ROWS : (2 * h + 1) * ROWS] = q[:, :, h * DH : (h + 1) * DH]


def gather_queries(q, arrived):
    return pl.pallas_call(
        gather_body,
        in_specs=[pl.BlockSpec(memory_space=pltpu.HBM), WHOLE],
        out_specs=WHOLE,
        out_shape=jax.ShapeDtypeStruct((SEQS, GROUP * 2 * ROWS, DH), jnp.bfloat16),
        scratch_shapes=[
            pltpu.VMEM((SEQS, ROWS, WIDE), jnp.bfloat16),
            pltpu.SemaphoreType.DMA,
        ],
        name="gather_queries",
        **params(),
    )(q, arrived)


def join(old, new, limit=DH):
    top = jnp.maximum(old[:, :limit], new[:, :limit])
    old_scale = jnp.exp2((old[:, :limit] - top) * EXP_SCALE)
    scale = jnp.exp2((new[:, :limit] - top) * EXP_SCALE)
    total = old_scale * old[:, DH : DH + limit] + scale * new[:, DH : DH + limit]
    return top, total, old_scale, scale


STATE = [
    jax.ShapeDtypeStruct((SEQS, 2 * ROWS, WIDE), jnp.float32),
    jax.ShapeDtypeStruct((SEQS, 2 * ROWS, 2 * DH), jnp.float32),
]
PARTIAL = [
    jax.ShapeDtypeStruct((4 * SEQS, 2 * ROWS, WIDE), jnp.float32),
    jax.ShapeDtypeStruct((4 * SEQS, 2 * ROWS, 2 * DH), jnp.float32),
]


def image_body(hops, plan, *refs):
    n = len(hops)
    chunks = refs[:n]
    query = refs[n]
    out, stat, token, keys, values = refs[-5:]
    token[...] = jnp.zeros_like(token)
    step = pl.program_id(0)

    @pl.when(step == 0)
    def _():
        values[:, DH:] = jnp.ones((VPAD, DH), jnp.bfloat16)
        values[VROWS:, :DH] = jnp.zeros((VPAD - VROWS, DH), jnp.bfloat16)
        keys[VROWS:, :] = jnp.zeros((VPAD - VROWS, DH), jnp.bfloat16)

    for i in range(n):

        @pl.when(step == i)
        def _(i=i):
            keys[:VROWS, :] = chunks[i][TEXT:, :DH]
            values[:VROWS, :DH] = chunks[i][TEXT:, DH:]

    place = pick(step, [plan[PLACE + source(plan, hop)] for hop in hops])
    visible = query_positions(plan) >= place
    lanes = lax.broadcasted_iota(jnp.int32, (1, DH), 1)

    def limit(scores):
        edge = jnp.where(lanes < VTOK - (VPAD - DH), scores[:, VPAD - DH :], NEG)
        return jnp.concatenate([scores[:, : VPAD - DH], edge], axis=1)

    rows = query[pick(step, [plan[OWNER + source(plan, hop)] for hop in hops])]
    k, v = keys[...].T, values[...]
    peaks, sums = attend([(some_heads(rows, heads), k, v) for heads in IMAGE_HEADS], limit)
    stat[0] = pack_stats([jnp.where(visible, peak, NEG) for peak in peaks], sums)
    for h in range(GROUP):
        out[0, :, h * DH : (h + 1) * DH] = sums[h][:, :DH]


TOKEN_SPEC = pl.BlockSpec((8, DH), lambda i, plan: (0, 0))


def image_part(plan, hops, chunks, query, held, mark):
    n = len(hops)

    def slot(i, plan):
        return (pick(i, [plan[SLOT + source(plan, hop)] for hop in hops]), 0, 0)

    out = pl.pallas_call(
        functools.partial(image_body, hops),
        grid_spec=pltpu.PrefetchScalarGridSpec(
            num_scalar_prefetch=1,
            grid=(n,),
            in_specs=[WHOLE] * (n + 1) + [ANYWHERE] * (1 + len(held)),
            out_specs=[pl.BlockSpec((1,) + a.shape[1:], slot) for a in PARTIAL] + [TOKEN_SPEC],
            scratch_shapes=[
                pltpu.VMEM((VPAD, DH), jnp.bfloat16),
                pltpu.VMEM((VPAD, 2 * DH), jnp.bfloat16),
            ],
        ),
        out_shape=PARTIAL + [TOKEN],
        input_output_aliases={n + 3: 0, n + 4: 1} if held else {},
        name="image_part",
        **params(),
    )(plan, *chunks, query, mark, *held)
    return out[:2], out[2]


def text_scores(plan, hops, chunks, query, seqs):
    n = len(hops)
    lanes = lax.broadcasted_iota(jnp.int32, (1, n * ROWS), 1)
    start = pick(lanes // ROWS, [plan[OFFSET + source(plan, hop)] for hop in hops])
    key_pos = start + lanes % ROWS
    visible = key_pos <= query_positions(plan)
    jobs = []
    for seq in seqs:
        mine = slice(seq * ROWS, (seq + 1) * ROWS)
        k = jnp.concatenate([r[mine, :DH] for r in chunks], axis=0).T
        v = jnp.concatenate([r[mine, DH:] for r in chunks], axis=0)
        v = jnp.concatenate([v, jnp.ones_like(v)], axis=1)
        jobs += [(some_heads(query[seq], heads), k, v) for heads in TEXT_HEADS]

    def limit(scores):
        count = scores.shape[0] // (2 * ROWS)
        scores = scores.reshape(count, 2 * ROWS, n * ROWS)
        return jnp.where(visible[None], scores, NEG).reshape(count * 2 * ROWS, n * ROWS)

    peaks, sums = attend(jobs, limit)
    cut = [slice(i * GROUP, (i + 1) * GROUP) for i in range(len(seqs))]
    return [(peaks[c], sums[c]) for c in cut]


def text_body(hops, plan, *refs):
    n = len(hops)
    held = refs[n + 2 : -3]
    out, stat, token = refs[-3:]
    token[...] = jnp.zeros_like(token)
    for seq, (peaks, sums) in enumerate(
        text_scores(plan, hops, refs[:n], refs[n], range(SEQS))
    ):
        stats = pack_stats(peaks, sums)
        if held:
            top, total, old_scale, scale = join(held[1][seq], stats)
            stats = jnp.concatenate([top, total], axis=1)
        stat[seq] = stats
        for h in range(GROUP):
            cols = slice(h * DH, (h + 1) * DH)
            value = sums[h][:, :DH]
            if held:
                value = old_scale[:, h : h + 1] * held[0][seq, :, cols] + scale[:, h : h + 1] * value
            out[seq, :, cols] = value


def text_part(plan, hops, chunks, query, held, mark):
    n = len(hops)
    out = pl.pallas_call(
        functools.partial(text_body, hops),
        grid_spec=pltpu.PrefetchScalarGridSpec(
            num_scalar_prefetch=1,
            grid=(1,),
            in_specs=[WHOLE] * (n + 1) + [ANYWHERE] + [WHOLE] * len(held),
            out_specs=[WHOLE] * 3,
        ),
        out_shape=STATE + [TOKEN],
        name="text_part",
        **params(),
    )(plan, *chunks, query, mark, *held)
    return out[:2], out[2]


def finish_body(hops, seqs, plan, *refs):
    n = len(hops)
    query, text, text_stat, visual, visual_stat, gate_own, gate_in = refs[n : n + 7]
    out, theirs = refs[-2:]
    group = 2 * plan[CORE] + plan[X]
    scored = text_scores(plan, hops, refs[:n], query, seqs)
    for row, (seq, (peaks, sums)) in enumerate(zip(seqs, scored)):
        logits = jnp.concatenate([gate_own[seq], gate_in[seq]], axis=0)
        logits = pick(group, [logits[:, g * GROUP : (g + 1) * GROUP] for g in range(4)])
        gate = 1.0 / (1.0 + jnp.exp(-logits))
        _, total, old_scale, scale = join(text_stat[seq], pack_stats(peaks, sums), GROUP)
        text_factor = (1.0 - gate) / total
        places = [4 * seq + j for j in range(4)]
        tops = [visual_stat[place, :, :GROUP] for place in places]
        top = functools.reduce(jnp.maximum, tops)
        scales = [jnp.exp2((a - top) * EXP_SCALE) for a in tops]
        totals = [a * visual_stat[i, :, DH : DH + GROUP] for a, i in zip(scales, places)]
        visual_factor = gate / sum(totals)
        factors = [text_factor * scale, text_factor * old_scale]
        factors += [visual_factor * a for a in scales]
        for h in range(GROUP):
            cols = slice(h * DH, (h + 1) * DH)
            values = [sums[h][:, :DH], text[seq, :, cols]] + [visual[i, :, cols] for i in places]
            mixed = sum(factor[:, h : h + 1] * value for factor, value in zip(factors, values))
            mixed = mixed.astype(jnp.bfloat16)
            out[row, :, cols] = mixed[:ROWS]
            theirs[row, :, cols] = mixed[ROWS:]


def finish(plan, hops, seqs, chunks, query, text, visual, gates, held):
    n, count = len(hops), len(seqs)
    block = seqs[0] // count
    mine = pl.BlockSpec((count, ROWS, WIDE), lambda i, plan: (block, 0, plan[X]))
    return pl.pallas_call(
        functools.partial(finish_body, hops, seqs),
        grid_spec=pltpu.PrefetchScalarGridSpec(
            num_scalar_prefetch=1,
            grid=(1,),
            in_specs=[WHOLE] * (n + 7) + [ANYWHERE] * len(held),
            out_specs=[mine, WHOLE],
        ),
        out_shape=[
            jax.ShapeDtypeStruct((SEQS, ROWS, 2 * WIDE), jnp.bfloat16),
            jax.ShapeDtypeStruct((count, ROWS, WIDE), jnp.bfloat16),
        ],
        input_output_aliases={n + 8: 0} if held else {},
        name="finish",
        **params(),
    )(plan, *chunks, query, *text, *visual, *gates, *held)


def place_body(plan, arrived, mine, out):
    del plan, mine
    out[...] = arrived[...]


def place(plan, seqs, arrived, mine):
    shape = (len(seqs), ROWS, WIDE)
    block = seqs[0] // len(seqs)
    return pl.pallas_call(
        place_body,
        grid_spec=pltpu.PrefetchScalarGridSpec(
            num_scalar_prefetch=1,
            grid=(1,),
            in_specs=[
                pl.BlockSpec(shape, lambda i, plan: (0, 0, 0)),
                pl.BlockSpec(memory_space=pl.ANY),
            ],
            out_specs=pl.BlockSpec(shape, lambda i, plan: (block, 0, 1 - plan[X])),
        ),
        out_shape=jax.ShapeDtypeStruct((SEQS, ROWS, 2 * WIDE), jnp.bfloat16),
        input_output_aliases={2: 0},
        name="place",
        **params(),
    )(plan, arrived, mine)


def on_device(
    queries,
    text_keys,
    text_values,
    visual_keys,
    visual_values,
    gate_weight,
    text_offsets,
    image_sequence,
    image_position,
):
    z, x, core = lax.axis_index("z"), lax.axis_index("x"), lax.axis_index("kvh")
    same = image_sequence[:, None] == image_sequence[None, :]
    before = jnp.arange(16)[:, None] > jnp.arange(16)[None, :]
    slot = image_sequence * 4 + jnp.sum(same & before, axis=1, dtype=jnp.int32)
    plan = jnp.concatenate(
        [
            jnp.stack([z, x, core]).astype(jnp.int32),
            text_offsets,
            image_sequence,
            image_position,
            slot,
        ]
    )
    swap = functools.partial(lax.ppermute, axis_name="x", perm=[(0, 1), (1, 0)])
    up = functools.partial(
        lax.ppermute, axis_name="z", perm=[(i, (i + 1) % PLANES) for i in range(PLANES)]
    )
    down = functools.partial(
        lax.ppermute, axis_name="z", perm=[(i, (i - 1) % PLANES) for i in range(PLANES)]
    )
    tie = lax.optimization_barrier
    own, other, half_q = pack(text_keys, text_values, visual_keys, visual_values, queries)
    got = {(0, 0): own}
    visual = ()
    text = ()

    def take(hops):
        return [got[hop] for hop in hops]

    mark = None

    def images(*hops):
        nonlocal visual, mark
        visual, mark = image_part(plan, list(hops), take(hops), query, visual, mark)

    def texts(*hops):
        nonlocal text, mark
        text, mark = text_part(plan, list(hops), take(hops), query, text, mark)

    def relay(plane, stream):
        nonlocal mark
        back, front = got[1 - plane, stream], got[plane - 1, stream]
        if mark is not None:
            back, front, mark = tie((back, front, mark))
        if plane < 4 or stream == 0:
            got[-plane, stream] = up(back)
        if plane < 4 or stream == 1:
            got[plane, stream] = down(front)

    relay(1, 0)
    got[0, 1] = swap(other)
    arrived = swap(half_q)
    relay(1, 1)
    query = gather_queries(queries, arrived)
    relay(2, 0)
    mark = query
    images((0, 0), (0, 1))
    relay(2, 1)
    images((-1, 0), (1, 0))
    share, mark = gate_share(queries, gate_weight, mark)
    logits = share + lax.ppermute(share, "kvh", [(0, 1), (1, 0)])
    relay(3, 0)
    images((-1, 1), (1, 1))
    images((-2, 0), (2, 0))
    relay(3, 1)
    mark, logits = tie((mark, logits))
    gates = (logits, swap(logits))
    images((-2, 1), (2, 1))
    texts((0, 0), (0, 1), (-1, 0), (1, 0), (-1, 1), (1, 1))
    relay(4, 0)
    images((-3, 0), (3, 0))
    mark, far_logits = tie((mark, gates[1]))
    gates = (logits, far_logits)
    relay(4, 1)
    images((-3, 1), (3, 1))
    texts((-2, 0), (2, 0), (-2, 1), (2, 1), (-3, 0), (3, 0), (-3, 1), (3, 1))
    images((-4, 0),)
    images((4, 1),)
    last = [(-4, 0), (4, 1)]
    state = (take(last), query, text, visual, gates)
    mine, theirs = finish(plan, last, (0, 1), *state, ())
    arrived = swap(theirs)
    mine, theirs = finish(plan, last, (2, 3), *state, (mine,))
    arrived_next = swap(theirs)
    mine = place(plan, (0, 1), arrived, mine)
    return place(plan, (2, 3), arrived_next, mine)


def solution(mesh):
    cut = Mesh(mesh.devices.reshape(PLANES, 2, 2, 8), ("z", "x", "kvh", "batch"))
    seq = ("z", "x")
    return jax.shard_map(
        on_device,
        mesh=cut,
        in_specs=(
            P("batch", seq, "kvh"),
            P("batch", seq, "kvh"),
            P("batch", seq, "kvh"),
            P(("batch",) + seq, None, "kvh"),
            P(("batch",) + seq, None, "kvh"),
            P("kvh", None),
            P("batch"),
            P("batch"),
            P("batch"),
        ),
        out_specs=P("batch", seq, "kvh"),
        check_vma=False,
    )
```

```python
import functools

import jax
import jax.numpy as jnp
from jax import lax
from jax.experimental import pallas as pl
from jax.experimental.pallas import tpu as pltpu
from jax.sharding import Mesh, PartitionSpec as P

HQ = 28
DH = 128
GROUP = 7
SEQS = 4
ROWS = 64
WIDE = GROUP * DH
VTOK = 729
VROWS = 736
VPAD = 768
TEXT = SEQS * ROWS
CHUNK = TEXT + VROWS
PLANES = 8
NEG = -1e30
EXP_SCALE = 1.4426950408889634 / DH**0.5

Z, X, CORE, OFFSET, OWNER, PLACE, SLOT = 0, 1, 2, 3, 19, 35, 51

VMEM_BYTES = 20 * 1024 * 1024
ALL_VMEM = 63 * 1024 * 1024
IMAGE_HEADS = [[0, 1], [2, 3], [4, 5], [6]]
TEXT_HEADS = [[0, 1, 2, 3], [4, 5, 6]]

TOKEN = jax.ShapeDtypeStruct((8, DH), jnp.float32)
WHOLE = pl.BlockSpec(memory_space=pltpu.VMEM)
ANYWHERE = pl.BlockSpec(memory_space=pl.ANY)


def source(plan, hop):
    plane, stream = hop
    z = lax.rem(plan[Z] + (plane + PLANES), PLANES)
    x = plan[X] if stream == 0 else 1 - plan[X]
    return 2 * z + x


def pick(step, options):
    value = options[0]
    for i in range(1, len(options)):
        value = jnp.where(step == i, options[i], value)
    return value


def params(vmem=VMEM_BYTES):
    return dict(
        compiler_params=pltpu.CompilerParams(vmem_limit_bytes=vmem),
        cost_estimate=pl.CostEstimate(flops=1000, bytes_accessed=1000, transcendentals=0),
    )


def some_heads(query, heads):
    return query[heads[0] * 2 * ROWS : (heads[-1] + 1) * 2 * ROWS]


def query_positions(plan):
    rows = lax.broadcasted_iota(jnp.int32, (2 * ROWS, 1), 0)
    own = plan[OFFSET + 2 * plan[Z] + plan[X]]
    other = plan[OFFSET + 2 * plan[Z] + 1 - plan[X]]
    return jnp.where(rows < ROWS, own + rows, other + rows - ROWS)


def pack_stats(peaks, sums):
    lanes = lax.broadcasted_iota(jnp.int32, (2 * ROWS, DH), 1)
    totals = [a[:, DH:] for a in sums]
    peak, total = peaks[0], totals[0]
    for h in range(1, GROUP):
        peak = jnp.where(lanes == h, peaks[h], peak)
        total = jnp.where(lanes == h, totals[h], total)
    return jnp.concatenate([peak, total], axis=1)


def attend(jobs, limit):
    def score(job):
        return jnp.dot(job[0], job[1], preferred_element_type=jnp.float32)

    peaks, sums = [], []
    ahead = score(jobs[0])
    for i, job in enumerate(jobs):
        scores = limit(ahead)
        if i + 1 < len(jobs):
            ahead = score(jobs[i + 1])
        peak = jnp.max(scores, axis=1, keepdims=True)
        weights = jnp.exp2((scores - peak) * EXP_SCALE).astype(jnp.bfloat16)
        summed = jnp.dot(weights, job[2], preferred_element_type=jnp.float32)
        for start in range(0, scores.shape[0], 2 * ROWS):
            peaks.append(peak[start : start + 2 * ROWS])
            sums.append(summed[start : start + 2 * ROWS])
    return peaks, sums


def pack_body(tk, tv, vk, vv, q, own, other, half_q, text, visual, sems):
    x = lax.axis_index("x")
    copies = [
        pltpu.make_async_copy(src, dst, sems.at[i])
        for i, (src, dst) in enumerate(
            [
                (tk, text.at[0]),
                (tv, text.at[1]),
                (vk, visual.at[0]),
                (vv, visual.at[1]),
                (q.at[:, :, pl.ds(pl.multiple_of((1 - x) * WIDE, DH), WIDE)], half_q),
            ]
        )
    ]
    for copy in copies:
        copy.start()
    for out in (own, other):
        out[CHUNK - 16 :, :] = jnp.zeros((16, 2 * DH), jnp.bfloat16)
    for copy in copies[:4]:
        copy.wait()
    for out, group in ((other, 1 - x), (own, x)):
        cols = pl.ds(pl.multiple_of(group * DH, DH), DH)
        for i in range(2):
            half = slice(i * DH, (i + 1) * DH)
            out[:TEXT, half] = text[i, :, :, cols].reshape(TEXT, DH)
            out[TEXT : TEXT + VTOK, half] = visual[i, 0, :, cols]
    copies[4].wait()


def pack(tk, tv, vk, vv, q):
    return pl.pallas_call(
        pack_body,
        in_specs=[pl.BlockSpec(memory_space=pltpu.HBM)] * 5,
        out_specs=[WHOLE] * 3,
        out_shape=[jax.ShapeDtypeStruct((CHUNK, 2 * DH), jnp.bfloat16)] * 2
        + [jax.ShapeDtypeStruct((SEQS, ROWS, WIDE), jnp.bfloat16)],
        scratch_shapes=[
            pltpu.VMEM((2, SEQS, ROWS, 2 * DH), jnp.bfloat16),
            pltpu.VMEM((2, 1, VTOK, 2 * DH), jnp.bfloat16),
            pltpu.SemaphoreType.DMA((5,)),
        ],
        name="pack",
        **params(ALL_VMEM),
    )(tk, tv, vk, vv, q)


def split3(total):
    hi = total.astype(jnp.bfloat16)
    rest = total - hi.astype(jnp.float32)
    mid = rest.astype(jnp.bfloat16)
    return hi, mid, (rest - mid.astype(jnp.float32)).astype(jnp.bfloat16)


def share_body(q, w, _, share, token):
    token[...] = jnp.zeros_like(token)
    rows = q[...].reshape(SEQS * ROWS, 2 * WIDE)
    acc = 0.0
    for part in reversed(split3(w[...])):
        acc += lax.dot_general(
            rows, part, (((1,), (1,)), ((), ())), preferred_element_type=jnp.float32
        )
    share[...] = acc.reshape(SEQS, ROWS, HQ)


def gate_share(q, w, mark):
    return pl.pallas_call(
        share_body,
        in_specs=[WHOLE] * 2 + [ANYWHERE],
        out_specs=[WHOLE] * 2,
        out_shape=[jax.ShapeDtypeStruct((SEQS, ROWS, HQ), jnp.float32), TOKEN],
        name="gate_share",
        **params(),
    )(q, w.T, mark)


def gather_body(q_all, arrived, query, q, sem):
    cols = pl.ds(pl.multiple_of(lax.axis_index("x") * WIDE, DH), WIDE)
    copy = pltpu.make_async_copy(q_all.at[:, :, cols], q, sem)
    copy.start()
    for h in range(GROUP):
        query[:, (2 * h + 1) * ROWS : (2 * h + 2) * ROWS] = arrived[:, :, h * DH : (h + 1) * DH]
    copy.wait()
    for h in range(GROUP):
        query[:, 2 * h * ROWS : (2 * h + 1) * ROWS] = q[:, :, h * DH : (h + 1) * DH]


def gather_queries(q, arrived):
    return pl.pallas_call(
        gather_body,
        in_specs=[pl.BlockSpec(memory_space=pltpu.HBM), WHOLE],
        out_specs=WHOLE,
        out_shape=jax.ShapeDtypeStruct((SEQS, GROUP * 2 * ROWS, DH), jnp.bfloat16),
        scratch_shapes=[
            pltpu.VMEM((SEQS, ROWS, WIDE), jnp.bfloat16),
            pltpu.SemaphoreType.DMA,
        ],
        name="gather_queries",
        **params(),
    )(q, arrived)


def join(old, new, limit=DH):
    top = jnp.maximum(old[:, :limit], new[:, :limit])
    old_scale = jnp.exp2((old[:, :limit] - top) * EXP_SCALE)
    scale = jnp.exp2((new[:, :limit] - top) * EXP_SCALE)
    total = old_scale * old[:, DH : DH + limit] + scale * new[:, DH : DH + limit]
    return top, total, old_scale, scale


STATE = [
    jax.ShapeDtypeStruct((SEQS, 2 * ROWS, WIDE), jnp.float32),
    jax.ShapeDtypeStruct((SEQS, 2 * ROWS, 2 * DH), jnp.float32),
]
PARTIAL = [
    jax.ShapeDtypeStruct((4 * SEQS, 2 * ROWS, WIDE), jnp.float32),
    jax.ShapeDtypeStruct((4 * SEQS, 2 * ROWS, 2 * DH), jnp.float32),
]


def image_body(hops, plan, *refs):
    n = len(hops)
    chunks = refs[:n]
    query = refs[n]
    out, stat, token, keys, values = refs[-5:]
    token[...] = jnp.zeros_like(token)
    step = pl.program_id(0)

    @pl.when(step == 0)
    def _():
        values[:, DH:] = jnp.ones((VPAD, DH), jnp.bfloat16)
        values[VROWS:, :DH] = jnp.zeros((VPAD - VROWS, DH), jnp.bfloat16)
        keys[VROWS:, :] = jnp.zeros((VPAD - VROWS, DH), jnp.bfloat16)

    for i in range(n):

        @pl.when(step == i)
        def _(i=i):
            keys[:VROWS, :] = chunks[i][TEXT:, :DH]
            values[:VROWS, :DH] = chunks[i][TEXT:, DH:]

    place = pick(step, [plan[PLACE + source(plan, hop)] for hop in hops])
    visible = query_positions(plan) >= place
    lanes = lax.broadcasted_iota(jnp.int32, (1, DH), 1)

    def limit(scores):
        edge = jnp.where(lanes < VTOK - (VPAD - DH), scores[:, VPAD - DH :], NEG)
        return jnp.concatenate([scores[:, : VPAD - DH], edge], axis=1)

    rows = query[pick(step, [plan[OWNER + source(plan, hop)] for hop in hops])]
    k, v = keys[...].T, values[...]
    peaks, sums = attend([(some_heads(rows, heads), k, v) for heads in IMAGE_HEADS], limit)
    stat[0] = pack_stats([jnp.where(visible, peak, NEG) for peak in peaks], sums)
    for h in range(GROUP):
        out[0, :, h * DH : (h + 1) * DH] = sums[h][:, :DH]


TOKEN_SPEC = pl.BlockSpec((8, DH), lambda i, plan: (0, 0))


def image_part(plan, hops, chunks, query, held, mark):
    n = len(hops)

    def slot(i, plan):
        return (pick(i, [plan[SLOT + source(plan, hop)] for hop in hops]), 0, 0)

    out = pl.pallas_call(
        functools.partial(image_body, hops),
        grid_spec=pltpu.PrefetchScalarGridSpec(
            num_scalar_prefetch=1,
            grid=(n,),
            in_specs=[WHOLE] * (n + 1) + [ANYWHERE] * (1 + len(held)),
            out_specs=[pl.BlockSpec((1,) + a.shape[1:], slot) for a in PARTIAL] + [TOKEN_SPEC],
            scratch_shapes=[
                pltpu.VMEM((VPAD, DH), jnp.bfloat16),
                pltpu.VMEM((VPAD, 2 * DH), jnp.bfloat16),
            ],
        ),
        out_shape=PARTIAL + [TOKEN],
        input_output_aliases={n + 3: 0, n + 4: 1} if held else {},
        name="image_part",
        **params(),
    )(plan, *chunks, query, mark, *held)
    return out[:2], out[2]


def text_scores(plan, hops, chunks, query, seqs):
    n = len(hops)
    lanes = lax.broadcasted_iota(jnp.int32, (1, n * ROWS), 1)
    start = pick(lanes // ROWS, [plan[OFFSET + source(plan, hop)] for hop in hops])
    key_pos = start + lanes % ROWS
    visible = key_pos <= query_positions(plan)
    jobs = []
    for seq in seqs:
        mine = slice(seq * ROWS, (seq + 1) * ROWS)
        k = jnp.concatenate([r[mine, :DH] for r in chunks], axis=0).T
        v = jnp.concatenate([r[mine, DH:] for r in chunks], axis=0)
        v = jnp.concatenate([v, jnp.ones_like(v)], axis=1)
        jobs += [(some_heads(query[seq], heads), k, v) for heads in TEXT_HEADS]

    def limit(scores):
        count = scores.shape[0] // (2 * ROWS)
        scores = scores.reshape(count, 2 * ROWS, n * ROWS)
        return jnp.where(visible[None], scores, NEG).reshape(count * 2 * ROWS, n * ROWS)

    peaks, sums = attend(jobs, limit)
    cut = [slice(i * GROUP, (i + 1) * GROUP) for i in range(len(seqs))]
    return [(peaks[c], sums[c]) for c in cut]


def text_body(hops, plan, *refs):
    n = len(hops)
    held = refs[n + 2 : -3]
    out, stat, token = refs[-3:]
    token[...] = jnp.zeros_like(token)
    for seq, (peaks, sums) in enumerate(
        text_scores(plan, hops, refs[:n], refs[n], range(SEQS))
    ):
        stats = pack_stats(peaks, sums)
        if held:
            top, total, old_scale, scale = join(held[1][seq], stats)
            stats = jnp.concatenate([top, total], axis=1)
        stat[seq] = stats
        for h in range(GROUP):
            cols = slice(h * DH, (h + 1) * DH)
            value = sums[h][:, :DH]
            if held:
                value = old_scale[:, h : h + 1] * held[0][seq, :, cols] + scale[:, h : h + 1] * value
            out[seq, :, cols] = value


def text_part(plan, hops, chunks, query, held, mark):
    n = len(hops)
    out = pl.pallas_call(
        functools.partial(text_body, hops),
        grid_spec=pltpu.PrefetchScalarGridSpec(
            num_scalar_prefetch=1,
            grid=(1,),
            in_specs=[WHOLE] * (n + 1) + [ANYWHERE] + [WHOLE] * len(held),
            out_specs=[WHOLE] * 3,
        ),
        out_shape=STATE + [TOKEN],
        name="text_part",
        **params(),
    )(plan, *chunks, query, mark, *held)
    return out[:2], out[2]


def finish_body(hops, seqs, plan, *refs):
    n = len(hops)
    query, text, text_stat, visual, visual_stat, gate_own, gate_in = refs[n : n + 7]
    out, theirs = refs[-2:]
    group = 2 * plan[CORE] + plan[X]
    scored = text_scores(plan, hops, refs[:n], query, seqs)
    for row, (seq, (peaks, sums)) in enumerate(zip(seqs, scored)):
        logits = jnp.concatenate([gate_own[seq], gate_in[seq]], axis=0)
        logits = pick(group, [logits[:, g * GROUP : (g + 1) * GROUP] for g in range(4)])
        gate = 1.0 / (1.0 + jnp.exp(-logits))
        _, total, old_scale, scale = join(text_stat[seq], pack_stats(peaks, sums), GROUP)
        text_factor = (1.0 - gate) / total
        places = [4 * seq + j for j in range(4)]
        tops = [visual_stat[place, :, :GROUP] for place in places]
        top = functools.reduce(jnp.maximum, tops)
        scales = [jnp.exp2((a - top) * EXP_SCALE) for a in tops]
        totals = [a * visual_stat[i, :, DH : DH + GROUP] for a, i in zip(scales, places)]
        visual_factor = gate / sum(totals)
        factors = [text_factor * scale, text_factor * old_scale]
        factors += [visual_factor * a for a in scales]
        for h in range(GROUP):
            cols = slice(h * DH, (h + 1) * DH)
            values = [sums[h][:, :DH], text[seq, :, cols]] + [visual[i, :, cols] for i in places]
            mixed = sum(factor[:, h : h + 1] * value for factor, value in zip(factors, values))
            mixed = mixed.astype(jnp.bfloat16)
            out[row, :, cols] = mixed[:ROWS]
            theirs[row, :, cols] = mixed[ROWS:]


def finish(plan, hops, seqs, chunks, query, text, visual, gates, held):
    n, count = len(hops), len(seqs)
    block = seqs[0] // count
    mine = pl.BlockSpec((count, ROWS, WIDE), lambda i, plan: (block, 0, plan[X]))
    return pl.pallas_call(
        functools.partial(finish_body, hops, seqs),
        grid_spec=pltpu.PrefetchScalarGridSpec(
            num_scalar_prefetch=1,
            grid=(1,),
            in_specs=[WHOLE] * (n + 7) + [ANYWHERE] * len(held),
            out_specs=[mine, WHOLE],
        ),
        out_shape=[
            jax.ShapeDtypeStruct((SEQS, ROWS, 2 * WIDE), jnp.bfloat16),
            jax.ShapeDtypeStruct((count, ROWS, WIDE), jnp.bfloat16),
        ],
        input_output_aliases={n + 8: 0} if held else {},
        name="finish",
        **params(),
    )(plan, *chunks, query, *text, *visual, *gates, *held)


def place_body(plan, arrived, mine, out):
    del plan, mine
    out[...] = arrived[...]


def place(plan, seqs, arrived, mine):
    shape = (len(seqs), ROWS, WIDE)
    block = seqs[0] // len(seqs)
    return pl.pallas_call(
        place_body,
        grid_spec=pltpu.PrefetchScalarGridSpec(
            num_scalar_prefetch=1,
            grid=(1,),
            in_specs=[
                pl.BlockSpec(shape, lambda i, plan: (0, 0, 0)),
                pl.BlockSpec(memory_space=pl.ANY),
            ],
            out_specs=pl.BlockSpec(shape, lambda i, plan: (block, 0, 1 - plan[X])),
        ),
        out_shape=jax.ShapeDtypeStruct((SEQS, ROWS, 2 * WIDE), jnp.bfloat16),
        input_output_aliases={2: 0},
        name="place",
        **params(),
    )(plan, arrived, mine)


def on_device(
    queries,
    text_keys,
    text_values,
    visual_keys,
    visual_values,
    gate_weight,
    text_offsets,
    image_sequence,
    image_position,
):
    z, x, core = lax.axis_index("z"), lax.axis_index("x"), lax.axis_index("kvh")
    same = image_sequence[:, None] == image_sequence[None, :]
    before = jnp.arange(16)[:, None] > jnp.arange(16)[None, :]
    slot = image_sequence * 4 + jnp.sum(same & before, axis=1, dtype=jnp.int32)
    plan = jnp.concatenate(
        [
            jnp.stack([z, x, core]).astype(jnp.int32),
            text_offsets,
            image_sequence,
            image_position,
            slot,
        ]
    )
    swap = functools.partial(lax.ppermute, axis_name="x", perm=[(0, 1), (1, 0)])
    up = functools.partial(
        lax.ppermute, axis_name="z", perm=[(i, (i + 1) % PLANES) for i in range(PLANES)]
    )
    down = functools.partial(
        lax.ppermute, axis_name="z", perm=[(i, (i - 1) % PLANES) for i in range(PLANES)]
    )
    tie = lax.optimization_barrier
    own, other, half_q = pack(text_keys, text_values, visual_keys, visual_values, queries)
    got = {(0, 0): own}
    visual = ()
    text = ()

    def take(hops):
        return [got[hop] for hop in hops]

    mark = None

    def images(*hops):
        nonlocal visual, mark
        visual, mark = image_part(plan, list(hops), take(hops), query, visual, mark)

    def texts(*hops):
        nonlocal text, mark
        text, mark = text_part(plan, list(hops), take(hops), query, text, mark)

    def relay(plane, stream):
        nonlocal mark
        back, front = got[1 - plane, stream], got[plane - 1, stream]
        if mark is not None:
            back, front, mark = tie((back, front, mark))
        if plane < 4 or stream == 0:
            got[-plane, stream] = up(back)
        if plane < 4 or stream == 1:
            got[plane, stream] = down(front)

    relay(1, 0)
    got[0, 1] = swap(other)
    arrived = swap(half_q)
    relay(1, 1)
    query = gather_queries(queries, arrived)
    relay(2, 0)
    mark = query
    images((0, 0), (0, 1))
    relay(2, 1)
    images((-1, 0), (1, 0))
    share, mark = gate_share(queries, gate_weight, mark)
    logits = share + lax.ppermute(share, "kvh", [(0, 1), (1, 0)])
    relay(3, 0)
    images((-1, 1), (1, 1))
    images((-2, 0), (2, 0))
    relay(3, 1)
    mark, logits = tie((mark, logits))
    gates = (logits, swap(logits))
    images((-2, 1), (2, 1))
    texts((0, 0), (0, 1), (-1, 0), (1, 0), (-1, 1), (1, 1))
    relay(4, 0)
    images((-3, 0), (3, 0))
    mark, far_logits = tie((mark, gates[1]))
    gates = (logits, far_logits)
    relay(4, 1)
    texts((-2, 0), (2, 0), (-2, 1), (2, 1), (-3, 0), (3, 0), (-3, 1), (3, 1))
    images((-3, 1), (3, 1), (-4, 0))
    images((4, 1),)
    last = [(-4, 0), (4, 1)]
    state = (take(last), query, text, visual, gates)
    mine, theirs = finish(plan, last, (0, 1), *state, ())
    arrived = swap(theirs)
    mine, theirs = finish(plan, last, (2, 3), *state, (mine,))
    arrived_next = swap(theirs)
    mine = place(plan, (0, 1), arrived, mine)
    return place(plan, (2, 3), arrived_next, mine)


def solution(mesh):
    cut = Mesh(mesh.devices.reshape(PLANES, 2, 2, 8), ("z", "x", "kvh", "batch"))
    seq = ("z", "x")
    return jax.shard_map(
        on_device,
        mesh=cut,
        in_specs=(
            P("batch", seq, "kvh"),
            P("batch", seq, "kvh"),
            P("batch", seq, "kvh"),
            P(("batch",) + seq, None, "kvh"),
            P(("batch",) + seq, None, "kvh"),
            P("kvh", None),
            P("batch"),
            P("batch"),
            P("batch"),
        ),
        out_specs=P("batch", seq, "kvh"),
        check_vma=False,
    )
```
